32 devices in a mesh: shard: 4 (over z), ctx: 4 (over x, core), tp: 2 (over y).
Axes of the slice: x: 2, y: 2, z: 4, core: 2. Of those that a mesh axis runs over, the one named last changes fastest.
Arguments:
- tokens: bfloat16 [4, 1024, 2048], P('shard', 'ctx'), may hold values from -6 to 6
- piece_starts: int32 [4, 2], P('shard'), may hold values from 0 to 768, as said below
- norm1_gain: bfloat16 [2048], P('shard'), may hold values from 0.25 to 1.75
- w_query: bfloat16 [2048, 2048], P('shard', 'tp'), may hold values from -0.1875 to 0.1875
- w_key: bfloat16 [2048, 2048], P('shard', 'tp'), may hold values from -0.1875 to 0.1875
- w_value: bfloat16 [2048, 2048], P('shard', 'tp'), may hold values from -0.125 to 0.125
- w_out: bfloat16 [2048, 2048], P('tp', 'shard'), may hold values from -0.5 to 0.5
- norm2_gain: bfloat16 [2048], P('shard'), may hold values from 0.25 to 1.75
- w_gate: bfloat16 [2048, 8192], P('shard', 'tp'), may hold values from -0.125 to 0.125
- w_up: bfloat16 [2048, 8192], P('shard', 'tp'), may hold values from -0.125 to 0.125
- w_down: bfloat16 [8192, 2048], P('tp', 'shard'), may hold values from -0.125 to 0.125
- cotangent: bfloat16 [4, 1024, 2048], P('shard', 'ctx'), may hold values from -6 to 6
Outputs:
- output: bfloat16 [4, 1024, 2048], P('shard', 'ctx')
- input_grad: bfloat16 [4, 1024, 2048], P('shard', 'ctx')
- grad_norm1: float32 [2048], P('shard')
- grad_query: float32 [2048, 2048], P('shard', 'tp')
- grad_key: float32 [2048, 2048], P('shard', 'tp')
- grad_value: float32 [2048, 2048], P('shard', 'tp')
- grad_out: float32 [2048, 2048], P('tp', 'shard')
- grad_norm2: float32 [2048], P('shard')
- grad_gate: float32 [2048, 8192], P('shard', 'tp')
- grad_up: float32 [2048, 8192], P('shard', 'tp')
- grad_down: float32 [8192, 2048], P('tp', 'shard')
The draws below stay inside these ranges and needn't reach their ends.
Inputs may be any that keep to these rules, and one draw needn't show every extreme that they name: `piece_starts`: piece k of a sequence (k from 0 to 1) starts between k * (512) and (k + 1) * 512 - 256, so that the pieces of a sequence never intersect.
All inputs are finite; a program needn't handle non-finite values.
Results may differ from the reference program's by a relative error of at most 0.018.
Values may be sent and summed in bfloat16 or wider, within the bound.
No kernel may reach another device: no remote copies, remote signals or barrier semaphores. Data moves between devices by JAX's collectives and lax.ppermute only.
A program may use at most 320 MiB of HBM per device.

```python
import math
import jax
import jax.numpy as jnp
from jax import lax

D = 2048
H = 32
HD = 64
FF = 8192
LEN = 1024
PIECE = 256
NPIECE = 2
SEQS = 4


def draw_piece_starts(key, part):
    region = LEN // NPIECE
    offsets = jax.random.randint(key, (SEQS, NPIECE), 0, region - PIECE + 1)
    bases = jnp.arange(NPIECE, dtype=jnp.int32) * region
    starts = bases[None, :] + offsets
    row_ids = jnp.arange(SEQS, dtype=jnp.int32)[:, None]
    col_ids = jnp.arange(NPIECE, dtype=jnp.int32)[None, :]
    starts = jnp.where((row_ids == 0) & (col_ids == 0), 0, starts)
    starts = jnp.where((row_ids == 0) & (col_ids == NPIECE - 1), LEN - PIECE, starts)
    return starts.astype(jnp.int32)


def strengthened(entries, own_key, source, target, shards_of, factor):
    owner, partner = [(jnp.arange(entries.shape[dim]) // (entries.shape[dim] // shards_of)).reshape([-1 if axis == dim else 1 for axis in range(entries.ndim)]) for dim in (source, target)]
    chosen = jax.random.permutation(own_key, shards_of)[partner]
    strong = (owner == chosen) | (owner == (partner + shards_of // 2) % shards_of)
    return jnp.where(strong, factor * entries, entries)


def block_levels(key, shape, split, least, high):
    level = 1.0
    for dim, shards_of in split:
        draws = jax.random.uniform(jax.random.fold_in(jax.random.fold_in(key, 6), dim), (shards_of,), jnp.float32, least / len(split), high / len(split))
        level = level * jnp.repeat(jnp.exp(draws), shape[dim] // shards_of).reshape((-1,) + (1,) * (len(shape) - 1 - dim))
    return level


def scatter_about(stream_key, shape, scale, limit, split=(), held_as=jnp.bfloat16):
    values = jax.random.normal(stream_key, shape, jnp.float32) * scale
    if len(split) > 0:
        values = block_levels(stream_key, shape, split, -0.22, 0.18) * values
    return jnp.clip(values, min=-limit, max=limit).astype(held_as)


def heavy_noise(stream_key, dims, scale, limit, cuts, heavy, kind=jnp.bfloat16):
    array = scale * jax.random.normal(stream_key, dims, jnp.float32)
    if cuts:
        array = array * block_levels(stream_key, dims, cuts, -0.22, 0.18)
    return jnp.clip(strengthened(array, jax.random.fold_in(stream_key, 3), *heavy), -limit, limit).astype(kind)


def setup_inputs(seed: int = 0) -> dict:
    key_list = jax.random.split(jax.random.key(seed), 13)
    return {
        "tokens": heavy_noise(key_list[0], (SEQS, LEN, D), 1.0, 6.0, ((0, 4), (1, 4)), (1, 2, 4, 2.0)),
        "piece_starts": draw_piece_starts(jax.random.fold_in(key_list[12], 71), 0),
        "norm1_gain": jnp.clip(1.0 + 0.15 * jax.random.normal(key_list[2], (D,), jnp.float32), 0.25, 1.75).astype(jnp.bfloat16),
        "w_query": scatter_about(key_list[3], (D, H * HD), (D // 2) ** -0.5, 0.1875, ((0, 4), (1, 2))),
        "w_key": scatter_about(key_list[4], (D, H * HD), (D // 2) ** -0.5, 0.1875, ((0, 4), (1, 2))),
        "w_value": scatter_about(key_list[5], (D, H * HD), D ** -0.5, 0.125, ((0, 4), (1, 2))),
        "w_out": scatter_about(key_list[6], (H * HD, D), (H * HD // 16) ** -0.5, 0.5, ((0, 2), (1, 4))),
        "norm2_gain": jnp.clip(1.0 + 0.15 * jax.random.normal(key_list[7], (D,), jnp.float32), 0.25, 1.75).astype(jnp.bfloat16),
        "w_gate": scatter_about(key_list[8], (D, FF), D ** -0.5, 0.125, ((0, 4), (1, 2))),
        "w_up": scatter_about(key_list[9], (D, FF), D ** -0.5, 0.125, ((0, 4), (1, 2))),
        "w_down": scatter_about(key_list[10], (FF, D), (FF // 4) ** -0.5, 0.125, ((0, 2), (1, 4))),
        "cotangent": heavy_noise(key_list[11], (SEQS, LEN, D), 1.0, 6.0, ((0, 4), (1, 4)), (0, 2, 4, 2.0)),
    }


@jax.custom_vjp
def low(v):
    return lax.optimization_barrier(v.astype(jnp.bfloat16)).astype(jnp.float32)

@jax.custom_vjp
def low_back(v):
    return v

def low_keep(v):
    return (low(v), None)

def low_pass(kept, grad):
    return (grad,)

def back_keep(v):
    return (v, None)

def back_low(kept, grad):
    return (low(grad),)
low.defvjp(low_keep, low_pass)
low_back.defvjp(back_keep, back_low)
epsilon = 1e-05
rope_base = 130000.0

def matmul_high(left, right):
    return jnp.dot(left, right, preferred_element_type=jnp.float32, precision=lax.Precision.HIGHEST)

def rms_norm(values, gain):
    factor = lax.rsqrt(lax.optimization_barrier(jnp.mean(values * values, axis=-1, keepdims=True)) + epsilon)
    return values * factor * gain

def rotate(values, positions):
    layout = values.shape
    halves = values.reshape(layout[:-1] + (layout[-1] // HD, 2, HD // 2))
    frequency = jnp.power(rope_base, -2.0 * jnp.arange(HD // 2, dtype=jnp.float32) / HD)
    angles = positions.astype(jnp.float32)[:, None] * frequency[None, :]
    cosine = jnp.cos(angles)[:, None, :]
    sine_table = jnp.sin(angles)[:, None, :]
    front_half = halves[..., 0, :]
    back_half = halves[..., 1, :]
    turned = jnp.stack([front_half * cosine - back_half * sine_table, back_half * cosine + front_half * sine_table], axis=-2)
    return turned.reshape(layout)

def visible(begins, length):
    places = jnp.arange(length, dtype=jnp.int32)
    inside = (places[None, :] >= begins[:, None]) & (places[None, :] < begins[:, None] + PIECE)
    shared = jnp.any(inside[:, :, None] & inside[:, None, :], axis=0)
    return (places[None, :] <= places[:, None]) | shared

def attend(packed):
    queries, keys, values, begins = packed
    length = queries.shape[0]
    score_scale = 1.0 / math.sqrt(HD)
    query_h = queries.reshape(length, H, HD)
    key_h = keys.reshape(length, H, HD)
    value_h = values.reshape(length, H, HD)
    scores = jnp.einsum('qhd,khd->hqk', query_h, key_h, precision=lax.Precision.HIGHEST) * score_scale
    scores = low_back(scores)
    scores = jnp.where(visible(begins, length)[None], scores, -1e+30)
    totals = jax.nn.logsumexp(scores, axis=-1, keepdims=True)
    probs = jnp.exp(scores - totals)
    mixed = jnp.einsum('hqk,khd->qhd', low(probs), value_h, precision=lax.Precision.HIGHEST)
    return mixed.reshape(length, H * HD)

def layer(weights, values, begins):
    norm1_gain, w_query, w_key, w_value, w_out, norm2_gain, w_gate, w_up, w_down = weights
    members = values.shape[0]
    places = jnp.arange(LEN, dtype=jnp.int32)
    token_rows = values.reshape(-1, D)
    normed = low(rms_norm(token_rows, norm1_gain))
    query = low(rotate(low_back(matmul_high(normed, w_query)).reshape(members, LEN, H * HD), places))
    key_rot = low(rotate(low_back(matmul_high(normed, w_key)).reshape(members, LEN, H * HD), places))
    value_all = low(low_back(matmul_high(normed, w_value))).reshape(members, LEN, H * HD)
    mixed = lax.map(jax.checkpoint(attend), (query, key_rot, value_all, begins))
    mixed = low(low_back(mixed)).reshape(-1, H * HD)
    after_attn = token_rows + low_back(matmul_high(mixed, w_out))
    normed_two = low(rms_norm(after_attn, norm2_gain))
    gate = low_back(matmul_high(normed_two, w_gate))
    up_proj = low_back(matmul_high(normed_two, w_up))
    hidden = low(jax.nn.silu(gate) * up_proj)
    result = after_attn + low_back(matmul_high(hidden, w_down))
    return result.reshape(values.shape)

def reference(tokens, piece_starts, norm1_gain, w_query, w_key, w_value, w_out, norm2_gain, w_gate, w_up, w_down, cotangent):
    params = tuple((weight.astype(jnp.float32) for weight in (norm1_gain, w_query, w_key, w_value, w_out, norm2_gain, w_gate, w_up, w_down)))
    group = max((members for members in range(1, SEQS + 1) if SEQS % members == 0 and members * LEN <= max(4096, LEN)))
    blocks = SEQS // group
    inputs = tokens.astype(jnp.float32).reshape(blocks, group, LEN, D)
    begins = piece_starts.astype(jnp.int32).reshape(blocks, group, NPIECE)
    seeds = cotangent.astype(jnp.float32).reshape(blocks, group, LEN, D)

    def advance(totals, packed):
        block_in, block_begins, block_seed = packed
        result, pull = jax.vjp(lambda weights, values: layer(weights, values, block_begins), params, block_in)
        grad_weights, grad_in = pull(block_seed)
        return (tuple((left + right for left, right in zip(totals, grad_weights))), (result, grad_in))
    start = tuple((jnp.zeros_like(weight) for weight in params))
    totals, (outputs, grads_in) = lax.scan(advance, start, (inputs, begins, seeds))
    return (outputs.reshape(SEQS, LEN, D).astype(jnp.bfloat16), grads_in.reshape(SEQS, LEN, D).astype(jnp.bfloat16), totals[0], totals[1], totals[2], totals[3], totals[4], totals[5], totals[6], totals[7], totals[8])
```

```python
import math

import jax
import jax.numpy as jnp
from jax import lax
from jax.sharding import PartitionSpec as P

HD = 64
PIECE = 256

EPS = 1e-05
ROPE_BASE = 130000.0
BF = jnp.bfloat16
F32 = jnp.float32


def flip(values, axis, bit, size):
    return lax.ppermute(values, axis, [(i, i ^ bit) for i in range(size)])


def bits_of(size):
    found, bit = [], size // 2
    while bit >= 1:
        found.append(bit)
        bit //= 2
    return found


def order_of(size):
    order = [0]
    for bit in bits_of(size):
        order = order + [o | bit for o in order]
    return order


def gather(block, axis, size):
    for bit in bits_of(size):
        block = jnp.concatenate([block, flip(block, axis, bit, size)], axis=0)
    return block


def reduce_blocks(partial, axis, size):
    for bit in reversed(bits_of(size)):
        half = partial.shape[0] // 2
        come = flip(partial[half:], axis, bit, size)
        partial = (partial[:half].astype(F32) + come.astype(F32)).astype(BF)
    return partial


def sum_tp(partial, size):
    for bit in bits_of(size):
        come = flip(partial, "tp", bit, size)
        partial = partial.astype(F32) + come.astype(F32)
        if bit > 1:
            partial = partial.astype(BF)
    return partial.astype(F32)


def mm(left, right):
    return jnp.dot(left, right, preferred_element_type=F32)


def mm_t(left, right):
    return lax.dot_general(left, right, (((0,), (0,)), ((), ())), preferred_element_type=F32)


def mm_nt(left, right):
    return lax.dot_general(left, right, (((1,), (1,)), ((), ())), preferred_element_type=F32)


def rope_tables(positions):
    frequency = jnp.power(ROPE_BASE, -2.0 * jnp.arange(HD // 2, dtype=F32) / HD)
    angles = positions.astype(F32)[:, None] * frequency[None, :]
    return jnp.cos(angles)[:, None, :], jnp.sin(angles)[:, None, :]


def rotate(values, cosine, sine):
    rows, columns = values.shape
    halves = values.reshape(rows, columns // HD, 2, HD // 2)
    front, back = halves[:, :, 0, :], halves[:, :, 1, :]
    turned = jnp.stack([front * cosine - back * sine, back * cosine + front * sine], axis=2)
    return turned.reshape(rows, columns)


def visible(begins, places):
    inside = (places[None, :] >= begins[:, None]) & (places[None, :] < begins[:, None] + PIECE)
    shared = jnp.any(inside[:, :, None] & inside[:, None, :], axis=0)
    return (places[None, :] <= places[:, None]) | shared


def heads_of(values):
    return values.reshape(values.shape[0], -1, HD)


def scores_of(query, key, seen):
    scores = jnp.einsum("qhd,khd->hqk", heads_of(query), heads_of(key), preferred_element_type=F32)
    return jnp.where(seen[None], scores * (1.0 / math.sqrt(HD)), -1e30)


def attend_forward(query, key, value, seen):
    scores = scores_of(query, key, seen)
    totals = jax.nn.logsumexp(scores, axis=-1, keepdims=True)
    weights = jnp.exp(scores - totals).astype(BF)
    mixed = jnp.einsum("hqk,khd->qhd", weights, heads_of(value), preferred_element_type=F32)
    return mixed.reshape(query.shape).astype(BF), totals


def attend_backward(query, key, value, seen, totals, grad, cosine, sine):
    scale = 1.0 / math.sqrt(HD)
    probs = jnp.exp(scores_of(query, key, seen) - totals)
    grad_h = heads_of(grad)
    grad_value = jnp.einsum("hqk,qhd->khd", probs.astype(BF), grad_h, preferred_element_type=F32)
    grad_probs = jnp.einsum("qhd,khd->hqk", grad_h, heads_of(value), preferred_element_type=F32)
    centre = jnp.sum(probs * grad_probs, axis=-1, keepdims=True)
    grad_scores = (probs * (grad_probs - centre)).astype(BF)
    grad_query = jnp.einsum("hqk,khd->qhd", grad_scores, heads_of(key), preferred_element_type=F32)
    grad_key = jnp.einsum("hqk,qhd->khd", grad_scores, heads_of(query), preferred_element_type=F32)
    grad_query = rotate(grad_query.reshape(query.shape) * scale, cosine, -sine)
    grad_key = rotate(grad_key.reshape(query.shape) * scale, cosine, -sine)
    return grad_query.astype(BF), grad_key.astype(BF), grad_value.reshape(query.shape).astype(BF)


def norm_forward(values, gain):
    factor = lax.rsqrt(jnp.mean(values * values, axis=-1, keepdims=True) + EPS)
    return values * factor, factor


def norm_backward(unit, factor, gain, grad):
    scaled = grad * gain
    back = factor * (scaled - unit * jnp.mean(scaled * unit, axis=-1, keepdims=True))
    return back, jnp.sum(grad * unit, axis=0)


def spread(share, index, size, axis):
    blocks = gather(share[None], "ctx", size)
    order = order_of(size)
    places = []
    for place in range(size):
        value = blocks[0]
        for at in range(1, size):
            value = jnp.where((index ^ order[at]) == place, blocks[at], value)
        places.append(value)
    return jnp.concatenate(places, axis=axis).astype(F32)


def body(n_shard, n_ctx, n_tp, *arguments):
    (tokens, piece_starts, gain1, w_query, w_key, w_value, w_out, gain2, w_gate, w_up, w_down, cotangent) = arguments
    sequences, rows, width = tokens.shape
    assert sequences == 1
    c = lax.axis_index("ctx")
    begins = piece_starts[0]
    places = jnp.concatenate([(c ^ o) * rows + jnp.arange(rows, dtype=jnp.int32) for o in order_of(n_ctx)])
    seen = visible(begins, places)
    cosine, sine = rope_tables(places)

    def columns_of(weight):
        share = weight.shape[1] // n_ctx
        return lax.dynamic_slice_in_dim(weight, c * share, share, axis=1)

    def rows_of(weight):
        share = weight.shape[0] // n_ctx
        return lax.dynamic_slice_in_dim(weight, c * share, share, axis=0)

    heads = w_query.shape[1] // n_ctx
    units = w_gate.shape[1] // n_ctx
    gains = lax.all_gather(jnp.stack([gain1, gain2]), "shard", axis=1, tiled=True).astype(F32)
    gain1_full, gain2_full = gains[0], gains[1]
    attn_pack = jnp.concatenate(
        [columns_of(w_query), columns_of(w_key), columns_of(w_value), rows_of(w_out).T], axis=1
    )
    attn_full = lax.all_gather(attn_pack, "shard", axis=0, tiled=True)
    wide_pack = jnp.concatenate([columns_of(w_gate), columns_of(w_up), rows_of(w_down).T], axis=1)
    wide_pack, attn_full = lax.optimization_barrier((wide_pack, attn_full))
    wide_full = lax.all_gather(wide_pack, "shard", axis=0, tiled=True)
    qkv_full, out_t = attn_full[:, : 3 * heads], attn_full[:, 3 * heads :]
    both_full, down_t = wide_full[:, : 2 * units], wide_full[:, 2 * units :]

    x = tokens[0].astype(F32)
    unit1, factor1 = norm_forward(x, gain1_full)
    n1 = gather((unit1 * gain1_full).astype(BF), "ctx", n_ctx)
    qkv = mm(n1, qkv_full)
    query = rotate(qkv[:, :heads], cosine, sine).astype(BF)
    key = rotate(qkv[:, heads : 2 * heads], cosine, sine).astype(BF)
    value = qkv[:, 2 * heads :].astype(BF)
    mixed, totals = attend_forward(query, key, value, seen)
    h1 = x + sum_tp(reduce_blocks(mm_nt(mixed, out_t).astype(BF), "ctx", n_ctx), n_tp)

    dy = gather(cotangent[0], "ctx", n_ctx)
    unit2, factor2 = norm_forward(h1, gain2_full)
    n2 = gather((unit2 * gain2_full).astype(BF), "ctx", n_ctx)
    both = mm(n2, both_full)
    gate, up = both[:, :units], both[:, units:]
    sigma = jax.nn.sigmoid(gate)
    silu = gate * sigma
    hidden = (silu * up).astype(BF)
    grad_down_t = mm_t(dy, hidden).astype(BF)
    grad_hidden = mm(dy, down_t)
    grad_gate = (grad_hidden * up * (sigma * (1.0 + gate * (1.0 - sigma)))).astype(BF)
    grad_up = (grad_hidden * silu).astype(BF)
    grad_both = jnp.concatenate([grad_gate, grad_up], axis=1)
    grad_both_w = mm_t(n2, grad_both).astype(BF)
    grad_n2 = sum_tp(reduce_blocks(mm_nt(grad_both, both_full).astype(BF), "ctx", n_ctx), n_tp)
    result = sum_tp(reduce_blocks(mm_nt(hidden, down_t).astype(BF), "ctx", n_ctx), n_tp)
    output = (h1 + result).astype(BF)[None]

    share_down = lax.psum_scatter(grad_down_t, "shard", scatter_dimension=0, tiled=True)
    share_both = lax.psum_scatter(grad_both_w, "shard", scatter_dimension=0, tiled=True)

    back2, grad_norm2 = norm_backward(unit2, factor2, gain2_full, grad_n2)
    grad_h1 = cotangent[0].astype(F32) + back2
    dh1 = gather(grad_h1.astype(BF), "ctx", n_ctx)
    grad_out_t = mm_t(dh1, mixed).astype(BF)
    grad_mixed = mm(dh1, out_t).astype(BF)
    dq, dk, dv = attend_backward(query, key, value, seen, totals, grad_mixed, cosine, sine)
    dqkv = jnp.concatenate([dq, dk, dv], axis=1)
    grad_attn = jnp.concatenate([mm_t(n1, dqkv).astype(BF), grad_out_t], axis=1)
    share_attn = lax.psum_scatter(grad_attn, "shard", scatter_dimension=0, tiled=True)
    grad_n1 = sum_tp(reduce_blocks(mm_nt(dqkv, qkv_full).astype(BF), "ctx", n_ctx), n_tp)
    back1, grad_norm1 = norm_backward(unit1, factor1, gain1_full, grad_n1)
    input_grad = (grad_h1 + back1).astype(BF)[None]

    norms = lax.psum(jnp.stack([grad_norm1, grad_norm2]), ("shard", "ctx"))
    share = width // n_shard
    norms = lax.dynamic_slice_in_dim(norms, lax.axis_index("shard") * share, share, axis=1)

    def spread_columns(values):
        return spread(values, c, n_ctx, 1)

    grad_q = spread_columns(share_attn[:, :heads])
    grad_k = spread_columns(share_attn[:, heads : 2 * heads])
    grad_v = spread_columns(share_attn[:, 2 * heads : 3 * heads])
    grad_o = spread(share_attn[:, 3 * heads :].T, c, n_ctx, 0)
    grad_g = spread_columns(share_both[:, :units])
    grad_u = spread_columns(share_both[:, units:])
    grad_d = spread(share_down.T, c, n_ctx, 0)
    return (output, input_grad, norms[0], grad_q, grad_k, grad_v, grad_o, norms[1], grad_g, grad_u, grad_d)


def solution(mesh):
    n_shard, n_ctx, n_tp = mesh.shape["shard"], mesh.shape["ctx"], mesh.shape["tp"]

    def local(*arguments):
        return body(n_shard, n_ctx, n_tp, *arguments)

    return jax.shard_map(
        local,
        mesh=mesh,
        in_specs=(
            P("shard", "ctx", None),
            P("shard", None),
            P("shard"),
            P("shard", "tp"),
            P("shard", "tp"),
            P("shard", "tp"),
            P("tp", "shard"),
            P("shard"),
            P("shard", "tp"),
            P("shard", "tp"),
            P("tp", "shard"),
            P("shard", "ctx", None),
        ),
        out_specs=(
            P("shard", "ctx", None),
            P("shard", "ctx", None),
            P("shard"),
            P("shard", "tp"),
            P("shard", "tp"),
            P("shard", "tp"),
            P("tp", "shard"),
            P("shard"),
            P("shard", "tp"),
            P("shard", "tp"),
            P("tp", "shard"),
        ),
        check_vma=False,
    )
```

```python
import math

import jax
import jax.numpy as jnp
from jax import lax
from jax.experimental import pallas as pl
from jax.experimental.pallas import tpu as pltpu
from jax.sharding import PartitionSpec as P

HD = 64
PIECE = 256

EPS = 1e-05
ROPE_BASE = 130000.0
BF = jnp.bfloat16
F32 = jnp.float32


def flip(values, axis, bit, size):
    return lax.ppermute(values, axis, [(i, i ^ bit) for i in range(size)])


def bits_of(size):
    found, bit = [], size // 2
    while bit >= 1:
        found.append(bit)
        bit //= 2
    return found


def order_of(size):
    order = [0]
    for bit in bits_of(size):
        order = order + [o | bit for o in order]
    return order


def tie(*values):
    return lax.optimization_barrier(values)


def gather(block, axis, size, dim=0):
    for bit in bits_of(size):
        block = jnp.concatenate([block, flip(block, axis, bit, size)], axis=dim)
    return block


def reduce_step(partial, axis, bit, size, dim=0):
    keep, give = jnp.split(partial, 2, axis=dim)
    come = flip(give, axis, bit, size)
    return (keep.astype(F32) + come.astype(F32)).astype(BF)


def mm(left, right):
    return jnp.dot(left, right, preferred_element_type=F32)


def mm_t(left, right):
    return lax.dot_general(left, right, (((0,), (0,)), ((), ())), preferred_element_type=F32)


def mm_nt(left, right):
    return lax.dot_general(left, right, (((1,), (1,)), ((), ())), preferred_element_type=F32)


def rope_tables(positions):
    frequency = jnp.power(ROPE_BASE, -2.0 * jnp.arange(HD // 2, dtype=F32) / HD)
    angles = positions.astype(F32)[:, None] * frequency[None, :]
    return jnp.cos(angles)[:, None, :], jnp.sin(angles)[:, None, :]


def rotate(values, cosine, sine):
    rows, columns = values.shape
    halves = values.reshape(rows, columns // HD, 2, HD // 2)
    front, back = halves[:, :, 0, :], halves[:, :, 1, :]
    turned = jnp.stack([front * cosine - back * sine, back * cosine + front * sine], axis=2)
    return turned.reshape(rows, columns)


def visible(begins, places):
    inside = (places[None, :] >= begins[:, None]) & (places[None, :] < begins[:, None] + PIECE)
    shared = jnp.any(inside[:, :, None] & inside[:, None, :], axis=0)
    return (places[None, :] <= places[:, None]) | shared


def attention_probs(query, key, bias):
    scores = mm_nt(query, key) * (1.0 / math.sqrt(HD)) + bias
    powers = jnp.exp(scores - jnp.max(scores, axis=-1, keepdims=True))
    return powers * (1.0 / jnp.sum(powers, axis=-1, keepdims=True))


def pair_specs(rows, count):
    return [pl.BlockSpec((rows, 2 * HD), lambda i: (0, i)) for _ in range(count)]


def attend_forward(query, key, value, bias):
    rows, columns = query.shape
    block = min(256, rows)

    def kernel(query_ref, key_ref, value_ref, bias_ref, out_ref):
        for head in range(2):
            lanes = slice(head * HD, (head + 1) * HD)
            k, v = key_ref[:, lanes], value_ref[:, lanes]
            for start in range(0, rows, block):
                now = slice(start, start + block)
                probs = attention_probs(query_ref[now, lanes], k, bias_ref[now, :])
                out_ref[now, lanes] = mm(probs.astype(BF), v).astype(BF)

    return pl.pallas_call(
        kernel,
        grid=(columns // (2 * HD),),
        in_specs=pair_specs(rows, 3) + [pl.BlockSpec((rows, rows), lambda i: (0, 0))],
        out_specs=pair_specs(rows, 1)[0],
        out_shape=jax.ShapeDtypeStruct((rows, columns), BF),
        compiler_params=pltpu.CompilerParams(vmem_limit_bytes=40 * 1024 * 1024),
        cost_estimate=pl.CostEstimate(
            flops=16 * rows * rows * columns,
            transcendentals=rows * rows * columns // HD,
            bytes_accessed=8 * rows * columns + 4 * rows * rows,
        ),
    )(query, key, value, bias)


def attend_backward(query, key, value, grad, bias, cosine, sine):
    rows, columns = query.shape
    block = min(256, rows)
    scale = 1.0 / math.sqrt(HD)

    def kernel(query_ref, key_ref, value_ref, grad_ref, bias_ref, cos_ref, sin_ref, dq_ref, dk_ref, dv_ref, q_acc, k_acc):
        lane = lax.broadcasted_iota(jnp.int32, (rows, 2 * HD), 1)
        front = lane % HD < HD // 2

        def turned_back(values):
            other = jnp.where(front, pltpu.roll(values, 2 * HD - HD // 2, 1), pltpu.roll(values, HD // 2, 1))
            return (values * cos_ref[...] + other * sin_ref[...]).astype(BF)

        for head in range(2):
            lanes = slice(head * HD, (head + 1) * HD)
            k, v = key_ref[:, lanes], value_ref[:, lanes]
            k_sum = jnp.zeros((HD, rows), F32)
            v_sum = jnp.zeros((HD, rows), F32)
            for start in range(0, rows, block):
                now = slice(start, start + block)
                q, g = query_ref[now, lanes], grad_ref[now, lanes]
                probs = attention_probs(q, k, bias_ref[now, :])
                v_sum += mm_t(g, probs.astype(BF))
                grad_probs = mm_nt(g, v)
                centre = jnp.sum(probs * grad_probs, axis=-1, keepdims=True)
                grad_scores = (probs * (grad_probs - centre)).astype(BF)
                q_acc[now, lanes] = mm(grad_scores, k) * scale
                k_sum += mm_t(q, grad_scores)
            k_acc[:, lanes] = k_sum.T * scale
            dv_ref[:, lanes] = v_sum.T.astype(BF)
        dq_ref[...] = turned_back(q_acc[...])
        dk_ref[...] = turned_back(k_acc[...])

    return pl.pallas_call(
        kernel,
        grid=(columns // (2 * HD),),
        in_specs=pair_specs(rows, 4)
        + [pl.BlockSpec((rows, rows), lambda i: (0, 0))]
        + [pl.BlockSpec((rows, 2 * HD), lambda i: (0, 0))] * 2,
        out_specs=pair_specs(rows, 3),
        out_shape=[jax.ShapeDtypeStruct((rows, columns), BF)] * 3,
        scratch_shapes=[pltpu.VMEM((rows, 2 * HD), F32)] * 2,
        compiler_params=pltpu.CompilerParams(vmem_limit_bytes=48 * 1024 * 1024),
        cost_estimate=pl.CostEstimate(
            flops=30 * rows * rows * columns,
            transcendentals=rows * rows * columns // HD,
            bytes_accessed=14 * rows * columns + 4 * rows * rows,
        ),
    )(query, key, value, grad, bias, cosine, sine)


def norm_forward(values):
    factor = lax.rsqrt(jnp.mean(values * values, axis=-1, keepdims=True) + EPS)
    return values * factor, factor


def norm_backward(unit, factor, gain, grad):
    scaled = grad * gain
    back = factor * (scaled - unit * jnp.mean(scaled * unit, axis=-1, keepdims=True))
    return back, jnp.sum(grad * unit, axis=0)


def place(pieces, targets, blocks, parts, axis):
    rows, columns = pieces[0].shape[0], pieces[0].shape[1] // parts
    total = len(pieces)

    def kernel(targets_ref, *refs):
        ins, outs = refs[:total], refs[total:]
        i = pl.program_id(0)
        for at, ref in enumerate(ins):

            @pl.when(i == at)
            def _():
                for j, out in enumerate(outs):
                    out[...] = ref[:, j * columns : (j + 1) * columns].astype(F32)

    def go(i, t):
        return (0, t[i]) if axis == 1 else (t[i], 0)

    shape = (rows, columns * blocks) if axis == 1 else (rows * blocks, columns)
    return pl.pallas_call(
        kernel,
        grid_spec=pltpu.PrefetchScalarGridSpec(
            num_scalar_prefetch=1,
            grid=(total,),
            in_specs=[pl.BlockSpec((rows, parts * columns), lambda i, t: (0, 0))] * total,
            out_specs=[pl.BlockSpec((rows, columns), go) for _ in range(parts)],
        ),
        out_shape=[jax.ShapeDtypeStruct(shape, F32) for _ in range(parts)],
        compiler_params=pltpu.CompilerParams(vmem_limit_bytes=32 * 1024 * 1024),
        cost_estimate=pl.CostEstimate(
            flops=0, transcendentals=0, bytes_accessed=6 * parts * rows * columns * blocks
        ),
    )(targets, *pieces)


def body(n_shard, n_ctx, n_tp, *arguments):
    (tokens, piece_starts, gain1, w_query, w_key, w_value, w_out, gain2, w_gate, w_up, w_down, cotangent) = arguments
    sequences, rows, width = tokens.shape
    assert sequences == 1
    z, c, t = lax.axis_index("shard"), lax.axis_index("ctx"), lax.axis_index("tp")
    short = rows // n_tp
    top = n_shard // 2
    high, low = z // top, z % top

    offsets = [(o, p) for o in order_of(n_ctx) for p in order_of(n_tp)]
    places = jnp.concatenate(
        [(c ^ o) * rows + (t ^ p) * short + jnp.arange(short, dtype=jnp.int32) for o, p in offsets]
    )
    bias = jnp.where(visible(piece_starts[0], places), 0.0, -1e30).astype(F32)
    cosine, sine = rope_tables(places)
    back_cosine = jnp.tile(cosine[:, 0, :], (1, 4))
    back_sine = jnp.tile(jnp.concatenate([sine[:, 0, :], -sine[:, 0, :]], axis=1), (1, 2))

    def own_first(values):
        return jnp.concatenate(
            [lax.dynamic_slice_in_dim(values, (t ^ p) * short, short, axis=0) for p in order_of(n_tp)]
        )

    def as_placed(found):
        result = jnp.zeros_like(found)
        for at, p in enumerate(order_of(n_tp)):
            block = found[at * short : (at + 1) * short]
            result = lax.dynamic_update_slice_in_dim(result, block, (t ^ p) * short, axis=0)
        return result[None]

    owners = jnp.stack([c ^ o for o in order_of(n_ctx)]).astype(jnp.int32)
    both_halves = jnp.concatenate([2 * owners + high, 2 * owners + 1 - high]).astype(jnp.int32)

    far_bits, tp_bits = bits_of(n_ctx)[:-1], bits_of(n_tp)
    chips = n_ctx // 2
    half = width // 2

    def halves(values, axis, bit, size, dim=0):
        keep, give = jnp.split(values, 2, axis=dim)
        return [keep, flip(give, axis, bit, size)]

    def added(keep, come):
        return (keep.astype(F32) + come.astype(F32)).astype(BF)

    def core_give(values):
        return halves(values, "ctx", 1, n_ctx)

    def ctx_give(values):
        for bit in reversed(far_bits[1:]):
            values = reduce_step(values, "ctx", bit, n_ctx)
        return halves(values, "ctx", far_bits[0], n_ctx)

    def tp_give(values, dim):
        for bit in reversed(tp_bits[1:]):
            values = reduce_step(values, "tp", bit, n_tp, dim)
        return halves(values, "tp", tp_bits[0], n_tp, dim)

    def first_give(values):
        right = values[:, half:].reshape(chips, n_tp * short, half)
        return ctx_give(values[:, :half]) + tp_give(right, 1)

    def last_give(keep, come, other_keep, other_come):
        right = added(other_keep, other_come).reshape(chips * short, half)
        return tp_give(added(keep, come), 0) + ctx_give(right)

    def reduced(keep, come, other_keep, other_come):
        return jnp.concatenate([added(keep, come), added(other_keep, other_come)], axis=1)

    def ctx_ask(values):
        for bit in far_bits[:-1]:
            values = jnp.concatenate([values, flip(values, "ctx", bit, n_ctx)], axis=0)
        return [values, flip(values, "ctx", far_bits[-1], n_ctx)]

    def tp_ask(values, dim):
        for bit in tp_bits[:-1]:
            values = jnp.concatenate([values, flip(values, "tp", bit, n_tp)], axis=dim)
        return [values, flip(values, "tp", tp_bits[-1], n_tp)]

    def first_ask(values):
        return tp_ask(values[:, :half], 0) + ctx_ask(values[:, half:])

    def last_ask(own, come, other_own, other_come):
        right = jnp.concatenate([other_own, other_come], axis=0).reshape(chips, short, half)
        return ctx_ask(jnp.concatenate([own, come], axis=0)) + tp_ask(right, 1)

    def joined(own, come, other_own, other_come):
        left = jnp.concatenate([own, come], axis=0)
        right = jnp.concatenate([other_own, other_come], axis=1).reshape(left.shape)
        return jnp.concatenate([left, right], axis=1)

    def core_ask(values):
        return [values, flip(values, "ctx", 1, n_ctx)]

    def stacked(*parts):
        return jnp.concatenate(parts, axis=0)

    def pair(values):
        return flip(values, "shard", top, n_shard)

    block = width // n_shard
    low_order = order_of(top)
    low_bits = bits_of(top)

    def folded(values):
        starts = [(side * top + (low ^ o)) * block for o in low_order for side in range(2)]
        return jnp.concatenate([lax.dynamic_slice_in_dim(values, s, block, axis=1) for s in starts], axis=1)

    def unfolded(values):
        where = jnp.asarray([low_order.index(o) for o in range(top)], jnp.int32)
        starts = [(2 * where[low ^ o] + side) * block for side in range(2) for o in range(top)]
        return jnp.concatenate([lax.dynamic_slice_in_dim(values, s, block, axis=1) for s in starts], axis=1)

    def low_ask(values):
        blocks = [values]
        for bit in low_bits:
            blocks = blocks + [flip(v, "shard", bit, n_shard) for v in blocks]
        return blocks

    def low_give(values, dim):
        for bit in reversed(low_bits[1:]):
            values = reduce_step(values, "shard", bit, n_shard, dim)
        return halves(values, "shard", low_bits[0], n_shard, dim)

    def packed(tied, *lengths):
        cuts, at = [], 0
        for length in lengths:
            cuts.append(list(tied[at : at + length]))
            at += length
        assert at == len(tied)
        return cuts

    def core_two(pieces):
        return pieces + [flip(v, "ctx", 1, n_ctx) for v in pieces]

    def ctx_two(values):
        pieces = [values]
        for bit in far_bits:
            pieces = pieces + [flip(v, "ctx", bit, n_ctx) for v in pieces]
        return pieces

    def swap(values, axis):
        size = values.shape[axis] // 2
        keep = lax.dynamic_slice_in_dim(values, high * size, size, axis=axis)
        give = lax.dynamic_slice_in_dim(values, (1 - high) * size, size, axis=axis)
        return keep, give

    heads = w_query.shape[1] // n_ctx
    units = w_gate.shape[1] // n_ctx // 2

    def attn_slice(weight, axis):
        return lax.dynamic_slice_in_dim(weight, c * heads, heads, axis=axis)

    def wide_slice(weight, side, axis):
        return lax.dynamic_slice_in_dim(weight, (2 * c + side) * units, units, axis=axis)

    attn_pack = [attn_slice(w, 1) for w in (w_query, w_key, w_value)] + [attn_slice(w_out, 0).T]
    attn_full = lax.all_gather(jnp.concatenate(attn_pack, axis=1), "shard", axis=0, tiled=True)
    gains = lax.all_gather(jnp.stack([gain1, gain2]), "shard", axis=1, tiled=True).astype(F32)
    gain1_full, gain2_full = gains[0], gains[1]
    x = own_first(tokens[0]).astype(F32)
    unit1, factor1 = norm_forward(x)
    n1 = gather((unit1 * gain1_full).astype(BF), "ctx", n_ctx)
    x, unit1, factor1 = x[:short], unit1[:short], factor1[:short]
    seed_all = own_first(cotangent[0])
    seed = seed_all[:short]
    seed_all = folded(seed_all)
    dy_pair = ctx_ask(seed_all)

    def ordered(own, come, axis):
        return jnp.where(
            high == 0,
            jnp.concatenate([own, come], axis=axis),
            jnp.concatenate([come, own], axis=axis),
        )

    give_gate, give_up = wide_slice(w_gate, 1 - high, 1), wide_slice(w_up, 1 - high, 1)
    give_down = wide_slice(w_down, 1 - high, 0)
    own_gate, own_up, own_down = wide_slice(w_gate, high, 1), wide_slice(w_up, high, 1), wide_slice(w_down, high, 0)
    dy_far = pair(seed_all[:short])
    attn_full, n1, dy_far, give_gate, give_up, give_down, *dy_near = tie(
        attn_full, n1, dy_far, give_gate, give_up, give_down, *dy_pair
    )

    qkv_full, out_full = attn_full[:, : 3 * heads], attn_full[:, 3 * heads :]
    come_gate = pair(give_gate)
    dy_far = first_ask(dy_far)
    qkv = mm(n1, qkv_full)
    query = rotate(qkv[:, :heads], cosine, sine).astype(BF)
    key = rotate(qkv[:, heads : 2 * heads], cosine, sine).astype(BF)
    value = qkv[:, 2 * heads :].astype(BF)
    mixed = attend_forward(query, key, value, bias)
    mixed, come_gate, give_up, give_down, *rest = tie(mixed, come_gate, give_up, give_down, *dy_far, *dy_near)
    dy_far, dy_near = rest[:4], rest[4:]
    come_up = pair(give_up)
    gate_blocks = low_ask(ordered(own_gate, come_gate, 0))
    partial = core_give(mm_nt(mixed, out_full).astype(BF))
    partial = first_give(added(*partial))
    partial = last_give(*tie(*partial))
    come_up, give_down, n1, *rest = tie(come_up, give_down, n1, *partial, *gate_blocks)
    partial, gate_blocks = rest[:4], rest[4:]
    up_blocks = low_ask(ordered(own_up, come_up, 0))
    h1 = x + reduced(*partial).astype(F32)
    unit2, factor2 = norm_forward(h1)
    n2_short = folded((unit2 * gain2_full).astype(BF))
    n2_far = pair(n2_short)
    near = first_ask(n2_short)
    *near, gate_full = tie(*near, stacked(*gate_blocks))
    near = last_ask(*near)
    n1_folded = folded(n1)
    dy_near = stacked(*dy_near)
    n2_far, give_down, n1_folded, gate_full, dy_near, *rest = tie(
        n2_far, give_down, n1_folded, gate_full, dy_near, *near, *up_blocks, *dy_far
    )
    near, up_blocks, dy_far = rest[:4], rest[4:-4], rest[-4:]

    come_down = pair(give_down)
    far = first_ask(n2_far)
    near = core_ask(joined(*near))
    up_full = stacked(*up_blocks)
    up_full, *rest = tie(up_full, *near, *far)
    near, far = rest[:2], rest[2:]
    wide_full = jnp.concatenate([gate_full, up_full], axis=1)
    n2_near = stacked(*near)

    def wide_forward(n2):
        both = mm(n2, wide_full)
        gate, up = both[:, :units], both[:, units:]
        sigma = jax.nn.sigmoid(gate)
        silu = gate * sigma
        return (silu * up).astype(BF), silu, up * (sigma * (1.0 + gate * (1.0 - sigma)))

    def wide_backward(dy, silu, slope):
        grad_hidden = mm_nt(dy, down_full)
        return (grad_hidden * slope).astype(BF), (grad_hidden * silu).astype(BF)

    def wide_input(grad_gate, grad_up):
        return mm_nt(jnp.concatenate([grad_gate, grad_up], axis=1), wide_full).astype(BF)

    far = last_ask(*far)
    forward_near = wide_forward(n2_near)
    come_down, n2_near, *rest = tie(come_down, n2_near, *forward_near, *far, *dy_far)
    forward_near, far, dy_far = rest[:3], rest[3:7], rest[7:]
    down_blocks = low_ask(ordered(own_down, come_down, 1))
    far = core_ask(joined(*far))
    dy_near = core_ask(dy_near)
    dy_far = last_ask(*dy_far)
    *far, dy_one, dy_two, one, two, three, four = tie(*far, *dy_near, *dy_far)
    dy_near = stacked(dy_one, dy_two)
    dy_far = core_ask(joined(one, two, three, four))
    n2_far = stacked(*far)
    forward_far = wide_forward(n2_far)
    n2_far, dy_near, *rest = tie(n2_far, dy_near, *forward_far, *dy_far, *down_blocks)
    forward_far, dy_far, down_full = rest[:3], rest[3:5], jnp.concatenate(rest[5:], axis=1)
    gate_near, up_near = wide_backward(dy_near, *forward_near[1:])
    near = wide_input(gate_near, up_near)
    near, gate_near, *dy_far = tie(near, gate_near, *dy_far)
    near = core_give(near)
    dy_far = stacked(*dy_far)
    gate_far, up_far = wide_backward(dy_far, *forward_far[1:])
    gate_far, up_far, dy_far, *near = tie(gate_far, up_far, dy_far, *near)
    near = first_give(added(*near))
    far = wide_input(gate_far, up_far)
    far, dy_far, n2_far, *near = tie(far, dy_far, n2_far, *near)
    far = core_give(far)
    near = last_give(*near)
    hidden = stacked(forward_near[0], forward_far[0])
    grad_down = mm_t(hidden, stacked(dy_near, dy_far)).astype(BF)
    grad_down, gate_near, *rest = tie(grad_down, gate_near, *far, *near)
    far, near = packed(rest, 2, 4)
    near = reduced(*near)
    far = first_give(added(*far))
    down_low = low_give(grad_down, 1)
    near, gate_near, n2_far, *far = tie(near, gate_near, n2_far, *far)
    far = last_give(*far)
    n2_both = stacked(n2_near, n2_far)
    grad_gate_w = mm_t(n2_both, stacked(gate_near, gate_far)).astype(BF)
    grad_gate_w, up_near, hidden, *rest = tie(grad_gate_w, up_near, hidden, *far, *down_low)
    far, down_low = packed(rest, 4, 2)

    far = pair(reduced(*far))
    down_keep, down_give = swap(added(*down_low), 1)
    down_keep = ctx_two(down_keep)
    grad_up_w = mm_t(n2_both, stacked(up_near, up_far)).astype(BF)
    grad_up_w, hidden = tie(grad_up_w, hidden)
    result = mm(hidden, down_full).astype(BF)
    far, grad_gate_w, grad_up_w, down_give, result, *down_keep = tie(
        far, grad_gate_w, grad_up_w, down_give, result, *down_keep
    )
    gate_low = low_give(grad_gate_w, 0)
    grad_n2 = unfolded(near.astype(F32) + far.astype(F32))
    back2, grad_norm2 = norm_backward(unit2, factor2, gain2_full, grad_n2)
    grad_h1 = seed.astype(F32) + back2
    dh1 = first_ask(grad_h1.astype(BF))
    down_give, *dh1 = tie(down_give, *dh1)
    dh1 = last_ask(*dh1)
    down_come = pair(down_give)
    result, grad_up_w, *rest = tie(result, grad_up_w, *dh1, *gate_low)
    dh1, gate_low = packed(rest, 4, 2)

    middle = result.shape[0] // 2
    dh1 = core_ask(joined(*dh1))
    result_near, result_far = core_give(result[:middle]), core_give(result[middle:])
    up_low = low_give(grad_up_w, 0)
    gate_keep, gate_give = swap(added(*gate_low), 0)
    gate_keep, gate_give, *rest = tie(gate_keep, gate_give, *dh1, *result_near, *result_far)
    dh1, result_near, result_far = packed(rest, 2, 2, 2)
    dh1, result_near = stacked(*dh1), added(*result_near)
    grad_out = mm_t(mixed, dh1).astype(BF)
    share_out = lax.psum_scatter(grad_out, "shard", scatter_dimension=1, tiled=True)
    dh1, grad_out = tie(dh1, grad_out)
    result_far = first_give(added(*result_far))
    grad_mixed = mm(dh1, out_full).astype(BF)
    grad_mixed, result_near, gate_keep, gate_give, down_come, *result_far = tie(
        grad_mixed, result_near, gate_keep, gate_give, down_come, *result_far
    )
    result_far = last_give(*result_far)
    gate_come = pair(gate_give)
    gate_keep, down_come = ctx_two(gate_keep), ctx_two(down_come)
    dq, dk, dv = attend_backward(query, key, value, grad_mixed, bias, back_cosine, back_sine)
    dq, dk, dv, gate_come, result_near, *rest = tie(
        dq, dk, dv, gate_come, result_near, *result_far, *gate_keep, *down_come, *up_low
    )
    result_far, gate_keep, down_come, up_low = packed(rest, 4, chips, chips, 2)
    dqkv = jnp.concatenate([dq, dk, dv], axis=1)
    grad_qkv = mm_t(n1_folded, dqkv).astype(BF)
    result_far = reduced(*result_far)
    up_keep, up_give = swap(added(*up_low), 0)

    dqkv, grad_qkv, gate_come, up_give, up_keep, share_out, result_near, result_far, *rest = tie(
        dqkv, grad_qkv, gate_come, up_give, up_keep, share_out, result_near, result_far, *gate_keep, *down_keep, *down_come
    )
    gate_keep, down_keep, down_come = packed(rest, chips, chips, chips)
    share_qkv = low_give(grad_qkv, 0)
    grad_n1 = core_give(mm_nt(dqkv, qkv_full).astype(BF))
    up_come = pair(up_give)
    result_near = first_give(result_near)
    gate_come, up_keep = ctx_two(gate_come), ctx_two(up_keep)
    down_pieces = core_two(down_keep) + core_two(down_come)
    up_come, share_out, result_far, *rest = tie(
        up_come, share_out, result_far,
        *share_qkv, *grad_n1, *result_near, *gate_come, *up_keep, *down_pieces, *gate_keep,
    )
    share_qkv, grad_n1, result_near, *rest = packed(rest, 2, 2, 4, chips, chips, 4 * chips, chips)
    gate_come, up_keep, down_pieces, gate_keep = rest
    share_qkv, qkv_give = swap(added(*share_qkv), 0)
    qkv_come = pair(qkv_give)
    grad_n1 = first_give(added(*grad_n1))
    up_come, share_out, result_far, *rest = tie(
        up_come, share_out, result_far, *grad_n1, *result_near, *down_pieces, *gate_keep, *gate_come, *up_keep
    )
    grad_n1, result_near, *rest = packed(rest, 4, 4, 4 * chips, chips, chips, chips)
    down_pieces, gate_keep, gate_come, up_keep = rest
    grad_n1 = last_give(*grad_n1)
    share_out = ctx_two(share_out)
    (grad_d,) = place(down_pieces, both_halves, 2 * n_ctx, 1, 0)
    grad_d, up_come, result_far, *rest = tie(
        grad_d, up_come, result_far, *grad_n1, *result_near, *share_out, *gate_keep, *gate_come, *up_keep
    )
    grad_n1, result_near, *rest = packed(rest, 4, 4, chips, chips, chips, chips)
    share_out, gate_keep, gate_come, up_keep = rest
    back1, grad_norm1 = norm_backward(unit1, factor1, gain1_full, reduced(*grad_n1).astype(F32))
    input_grad = tp_ask((grad_h1 + back1).astype(BF), 0)
    up_come = ctx_two(up_come)
    gate_pieces = core_two(gate_keep) + core_two(gate_come)
    share_qkv, qkv_come, result_far, grad_norm1, *rest = tie(
        share_qkv, qkv_come, result_far, grad_norm1, *input_grad, *result_near, *up_come, *gate_pieces, *up_keep, *share_out
    )
    input_grad, result_near, *rest = packed(rest, 2, 4, chips, 4 * chips, chips, chips)
    up_come, gate_pieces, up_keep, share_out = rest
    share_qkv = ctx_two(added(share_qkv, qkv_come))
    result_far = pair(result_far)
    result_near = last_give(*result_near)
    input_grad = as_placed(stacked(*input_grad))
    (grad_g,) = place(gate_pieces, both_halves, 2 * n_ctx, 1, 1)
    grad_g, result_far, input_grad, *rest = tie(
        grad_g, result_far, input_grad, *share_qkv, *result_near, *up_come, *up_keep, *share_out
    )
    share_qkv, result_near, up_come, up_keep, share_out = packed(rest, chips, 4, chips, chips, chips)
    qkv_pieces, out_pieces = core_two(share_qkv), core_two(share_out)
    up_pieces = core_two(up_keep) + core_two(up_come)
    output = h1 + unfolded(reduced(*result_near).astype(F32) + result_far.astype(F32))
    output = as_placed(stacked(*tp_ask(output.astype(BF), 0)))

    norms = jnp.stack([grad_norm1, grad_norm2]).reshape(-1, 128)
    for axis, size in (("tp", n_tp), ("ctx", n_ctx), ("shard", n_shard)):
        for bit in bits_of(size):
            norms = norms + flip(norms, axis, bit, size)
    norms = lax.dynamic_slice_in_dim(norms.reshape(2, width), z * block, block, axis=1)

    (grad_u,) = place(up_pieces, both_halves, 2 * n_ctx, 1, 1)
    (grad_o,) = place(out_pieces, owners, n_ctx, 1, 0)
    grad_q, grad_k, grad_v = place(qkv_pieces, owners, n_ctx, 3, 1)
    return (output, input_grad, norms[0], grad_q, grad_k, grad_v, grad_o, norms[1], grad_g, grad_u, grad_d)


def solution(mesh):
    n_shard, n_ctx, n_tp = mesh.shape["shard"], mesh.shape["ctx"], mesh.shape["tp"]

    def local(*arguments):
        return body(n_shard, n_ctx, n_tp, *arguments)

    return jax.shard_map(
        local,
        mesh=mesh,
        in_specs=(
            P("shard", "ctx", None),
            P("shard", None),
            P("shard"),
            P("shard", "tp"),
            P("shard", "tp"),
            P("shard", "tp"),
            P("tp", "shard"),
            P("shard"),
            P("shard", "tp"),
            P("shard", "tp"),
            P("tp", "shard"),
            P("shard", "ctx", None),
        ),
        out_specs=(
            P("shard", "ctx", None),
            P("shard", "ctx", None),
            P("shard"),
            P("shard", "tp"),
            P("shard", "tp"),
            P("shard", "tp"),
            P("tp", "shard"),
            P("shard"),
            P("shard", "tp"),
            P("shard", "tp"),
            P("tp", "shard"),
        ),
        check_vma=False,
    )
```

```python
import math

import jax
import jax.numpy as jnp
from jax import lax
from jax.experimental import pallas as pl
from jax.experimental.pallas import tpu as pltpu
from jax.sharding import PartitionSpec as P

HD = 64
PIECE = 256

EPS = 1e-05
ROPE_BASE = 130000.0
BF = jnp.bfloat16
F32 = jnp.float32


def flip(values, axis, bit, size):
    return lax.ppermute(values, axis, [(i, i ^ bit) for i in range(size)])


def bits_of(size):
    found, bit = [], size // 2
    while bit >= 1:
        found.append(bit)
        bit //= 2
    return found


def order_of(size):
    order = [0]
    for bit in bits_of(size):
        order = order + [o | bit for o in order]
    return order


def tie(*values):
    return lax.optimization_barrier(values)


def gather(block, axis, size, dim=0):
    for bit in bits_of(size):
        block = jnp.concatenate([block, flip(block, axis, bit, size)], axis=dim)
    return block


def reduce_step(partial, axis, bit, size, dim=0):
    keep, give = jnp.split(partial, 2, axis=dim)
    come = flip(give, axis, bit, size)
    return (keep.astype(F32) + come.astype(F32)).astype(BF)


def mm(left, right):
    return jnp.dot(left, right, preferred_element_type=F32)


def mm_t(left, right):
    return lax.dot_general(left, right, (((0,), (0,)), ((), ())), preferred_element_type=F32)


def mm_nt(left, right):
    return lax.dot_general(left, right, (((1,), (1,)), ((), ())), preferred_element_type=F32)


def rope_tables(positions):
    frequency = jnp.power(ROPE_BASE, -2.0 * jnp.arange(HD // 2, dtype=F32) / HD)
    angles = positions.astype(F32)[:, None] * frequency[None, :]
    return jnp.cos(angles)[:, None, :], jnp.sin(angles)[:, None, :]


def rotate(values, cosine, sine):
    rows, columns = values.shape
    halves = values.reshape(rows, columns // HD, 2, HD // 2)
    front, back = halves[:, :, 0, :], halves[:, :, 1, :]
    turned = jnp.stack([front * cosine - back * sine, back * cosine + front * sine], axis=2)
    return turned.reshape(rows, columns)


def visible(begins, places):
    inside = (places[None, :] >= begins[:, None]) & (places[None, :] < begins[:, None] + PIECE)
    shared = jnp.any(inside[:, :, None] & inside[:, None, :], axis=0)
    return (places[None, :] <= places[:, None]) | shared


def attention_probs(query, key, bias):
    scores = mm_nt(query, key) * (1.0 / math.sqrt(HD)) + bias
    powers = jnp.exp(scores - jnp.max(scores, axis=-1, keepdims=True))
    return powers * (1.0 / jnp.sum(powers, axis=-1, keepdims=True))


def pair_specs(rows, count):
    return [pl.BlockSpec((rows, 2 * HD), lambda i: (0, i)) for _ in range(count)]


def attend_forward(query, key, value, bias):
    rows, columns = query.shape
    block = min(256, rows)

    def kernel(query_ref, key_ref, value_ref, bias_ref, out_ref):
        for head in range(2):
            lanes = slice(head * HD, (head + 1) * HD)
            k, v = key_ref[:, lanes], value_ref[:, lanes]
            for start in range(0, rows, block):
                now = slice(start, start + block)
                probs = attention_probs(query_ref[now, lanes], k, bias_ref[now, :])
                out_ref[now, lanes] = mm(probs.astype(BF), v).astype(BF)

    return pl.pallas_call(
        kernel,
        grid=(columns // (2 * HD),),
        in_specs=pair_specs(rows, 3) + [pl.BlockSpec((rows, rows), lambda i: (0, 0))],
        out_specs=pair_specs(rows, 1)[0],
        out_shape=jax.ShapeDtypeStruct((rows, columns), BF),
        compiler_params=pltpu.CompilerParams(vmem_limit_bytes=40 * 1024 * 1024),
        cost_estimate=pl.CostEstimate(
            flops=16 * rows * rows * columns,
            transcendentals=rows * rows * columns // HD,
            bytes_accessed=8 * rows * columns + 4 * rows * rows,
        ),
    )(query, key, value, bias)


def attend_backward(query, key, value, grad, bias, cosine, sine):
    rows, columns = query.shape
    block = min(256, rows)
    scale = 1.0 / math.sqrt(HD)

    def kernel(query_ref, key_ref, value_ref, grad_ref, bias_ref, cos_ref, sin_ref, dq_ref, dk_ref, dv_ref, q_acc, k_acc):
        lane = lax.broadcasted_iota(jnp.int32, (rows, 2 * HD), 1)
        front = lane % HD < HD // 2

        def turned_back(values):
            other = jnp.where(front, pltpu.roll(values, 2 * HD - HD // 2, 1), pltpu.roll(values, HD // 2, 1))
            return (values * cos_ref[...] + other * sin_ref[...]).astype(BF)

        for head in range(2):
            lanes = slice(head * HD, (head + 1) * HD)
            k, v = key_ref[:, lanes], value_ref[:, lanes]
            k_sum = jnp.zeros((HD, rows), F32)
            v_sum = jnp.zeros((HD, rows), F32)
            for start in range(0, rows, block):
                now = slice(start, start + block)
                q, g = query_ref[now, lanes], grad_ref[now, lanes]
                probs = attention_probs(q, k, bias_ref[now, :])
                v_sum += mm_t(g, probs.astype(BF))
                grad_probs = mm_nt(g, v)
                centre = jnp.sum(probs * grad_probs, axis=-1, keepdims=True)
                grad_scores = (probs * (grad_probs - centre)).astype(BF)
                q_acc[now, lanes] = mm(grad_scores, k) * scale
                k_sum += mm_t(q, grad_scores)
            k_acc[:, lanes] = k_sum.T * scale
            dv_ref[:, lanes] = v_sum.T.astype(BF)
        dq_ref[...] = turned_back(q_acc[...])
        dk_ref[...] = turned_back(k_acc[...])

    return pl.pallas_call(
        kernel,
        grid=(columns // (2 * HD),),
        in_specs=pair_specs(rows, 4)
        + [pl.BlockSpec((rows, rows), lambda i: (0, 0))]
        + [pl.BlockSpec((rows, 2 * HD), lambda i: (0, 0))] * 2,
        out_specs=pair_specs(rows, 3),
        out_shape=[jax.ShapeDtypeStruct((rows, columns), BF)] * 3,
        scratch_shapes=[pltpu.VMEM((rows, 2 * HD), F32)] * 2,
        compiler_params=pltpu.CompilerParams(vmem_limit_bytes=48 * 1024 * 1024),
        cost_estimate=pl.CostEstimate(
            flops=30 * rows * rows * columns,
            transcendentals=rows * rows * columns // HD,
            bytes_accessed=14 * rows * columns + 4 * rows * rows,
        ),
    )(query, key, value, grad, bias, cosine, sine)


def norm_forward(values):
    factor = lax.rsqrt(jnp.mean(values * values, axis=-1, keepdims=True) + EPS)
    return values * factor, factor


def norm_backward(unit, factor, gain, grad):
    scaled = grad * gain
    back = factor * (scaled - unit * jnp.mean(scaled * unit, axis=-1, keepdims=True))
    return back, jnp.sum(grad * unit, axis=0)


def place(pieces, targets, blocks, parts, axis):
    rows, columns = pieces[0][0].shape[1], pieces[0][0].shape[2] // parts
    total = len(pieces)

    def kernel(targets_ref, *refs):
        ins, outs = refs[:total], refs[total:]
        i = pl.program_id(0)
        for at, ref in enumerate(ins):

            @pl.when(i == at)
            def _():
                for j, out in enumerate(outs):
                    out[...] = ref[:, j * columns : (j + 1) * columns].astype(F32)

    def go(i, t):
        return (0, t[i]) if axis == 1 else (t[i], 0)

    shape = (rows, columns * blocks) if axis == 1 else (rows * blocks, columns)
    return pl.pallas_call(
        kernel,
        grid_spec=pltpu.PrefetchScalarGridSpec(
            num_scalar_prefetch=1,
            grid=(total,),
            in_specs=[
                pl.BlockSpec((None, rows, parts * columns), lambda i, t, at=at: (at, 0, 0)) for _, at in pieces
            ],
            out_specs=[pl.BlockSpec((rows, columns), go) for _ in range(parts)],
        ),
        out_shape=[jax.ShapeDtypeStruct(shape, F32) for _ in range(parts)],
        compiler_params=pltpu.CompilerParams(vmem_limit_bytes=32 * 1024 * 1024),
        cost_estimate=pl.CostEstimate(
            flops=0, transcendentals=0, bytes_accessed=6 * parts * rows * columns * blocks
        ),
    )(targets, *[array for array, _ in pieces])


def body(n_shard, n_ctx, n_tp, *arguments):
    (tokens, piece_starts, gain1, w_query, w_key, w_value, w_out, gain2, w_gate, w_up, w_down, cotangent) = arguments
    sequences, rows, width = tokens.shape
    assert sequences == 1
    z, c, t = lax.axis_index("shard"), lax.axis_index("ctx"), lax.axis_index("tp")
    short = rows // n_tp
    top = n_shard // 2
    high, low = z // top, z % top

    offsets = [(o, p) for o in order_of(n_ctx) for p in order_of(n_tp)]
    places = jnp.concatenate(
        [(c ^ o) * rows + (t ^ p) * short + jnp.arange(short, dtype=jnp.int32) for o, p in offsets]
    )
    bias = jnp.where(visible(piece_starts[0], places), 0.0, -1e30).astype(F32)
    cosine, sine = rope_tables(places)
    back_cosine = jnp.tile(cosine[:, 0, :], (1, 4))
    back_sine = jnp.tile(jnp.concatenate([sine[:, 0, :], -sine[:, 0, :]], axis=1), (1, 2))

    def own_first(values):
        return jnp.concatenate(
            [lax.dynamic_slice_in_dim(values, (t ^ p) * short, short, axis=0) for p in order_of(n_tp)]
        )

    def as_placed(found):
        result = jnp.zeros_like(found)
        for at, p in enumerate(order_of(n_tp)):
            block = found[at * short : (at + 1) * short]
            result = lax.dynamic_update_slice_in_dim(result, block, (t ^ p) * short, axis=0)
        return result[None]

    owners = jnp.stack([c ^ o for o in order_of(n_ctx)]).astype(jnp.int32)
    both_halves = jnp.concatenate([2 * owners + high, 2 * owners + 1 - high]).astype(jnp.int32)

    far_bits, tp_bits = bits_of(n_ctx)[:-1], bits_of(n_tp)
    chips = n_ctx // 2
    half = width // 2

    def halves(values, axis, bit, size, dim=0):
        keep, give = jnp.split(values, 2, axis=dim)
        return [keep, flip(give, axis, bit, size)]

    def added(keep, come):
        return (keep.astype(F32) + come.astype(F32)).astype(BF)

    def core_give(values):
        return halves(values, "ctx", 1, n_ctx)

    def ctx_give(values):
        for bit in reversed(far_bits[1:]):
            values = reduce_step(values, "ctx", bit, n_ctx)
        return halves(values, "ctx", far_bits[0], n_ctx)

    def tp_give(values, dim):
        for bit in reversed(tp_bits[1:]):
            values = reduce_step(values, "tp", bit, n_tp, dim)
        return halves(values, "tp", tp_bits[0], n_tp, dim)

    def first_give(left, right=None):
        if right is None:
            left, right = left[:, :half], left[:, half:]
        return ctx_give(left) + tp_give(right.reshape(chips, n_tp * short, right.shape[1]), 1)

    def last_give(keep, come, other_keep, other_come):
        right = added(other_keep, other_come).reshape(chips * short, keep.shape[1])
        return tp_give(added(keep, come), 0) + ctx_give(right)

    def reduced(keep, come, other_keep, other_come):
        return jnp.concatenate([added(keep, come), added(other_keep, other_come)], axis=1)

    def ctx_ask(values):
        for bit in far_bits[:-1]:
            values = jnp.concatenate([values, flip(values, "ctx", bit, n_ctx)], axis=0)
        return [values, flip(values, "ctx", far_bits[-1], n_ctx)]

    def tp_ask(values, dim):
        for bit in tp_bits[:-1]:
            values = jnp.concatenate([values, flip(values, "tp", bit, n_tp)], axis=dim)
        return [values, flip(values, "tp", tp_bits[-1], n_tp)]

    def first_ask(values):
        return tp_ask(values[:, :half], 0) + ctx_ask(values[:, half:])

    def last_ask(own, come, other_own, other_come):
        right = jnp.concatenate([other_own, other_come], axis=0).reshape(chips, short, half)
        return ctx_ask(jnp.concatenate([own, come], axis=0)) + tp_ask(right, 1)

    def joined(own, come, other_own, other_come):
        left = jnp.concatenate([own, come], axis=0)
        right = jnp.concatenate([other_own, other_come], axis=1).reshape(left.shape)
        return jnp.concatenate([left, right], axis=1)

    def core_ask(values):
        return [values, flip(values, "ctx", 1, n_ctx)]

    def stacked(*parts):
        return jnp.concatenate(parts, axis=0)

    def pair(values):
        return flip(values, "shard", top, n_shard)

    block = width // n_shard
    low_order = order_of(top)
    low_bits = bits_of(top)

    def folded(values):
        starts = [(side * top + (low ^ o)) * block for o in low_order for side in range(2)]
        return jnp.concatenate([lax.dynamic_slice_in_dim(values, s, block, axis=1) for s in starts], axis=1)

    def unfolded(values):
        where = jnp.asarray([low_order.index(o) for o in range(top)], jnp.int32)
        starts = [(2 * where[low ^ o] + side) * block for side in range(2) for o in range(top)]
        return jnp.concatenate([lax.dynamic_slice_in_dim(values, s, block, axis=1) for s in starts], axis=1)

    def low_ask(values):
        blocks = [values]
        for bit in low_bits:
            blocks = blocks + [flip(v, "shard", bit, n_shard) for v in blocks]
        return blocks

    def low_give(values, dim):
        for bit in reversed(low_bits[1:]):
            values = reduce_step(values, "shard", bit, n_shard, dim)
        return halves(values, "shard", low_bits[0], n_shard, dim)

    def packed(tied, *lengths):
        cuts, at = [], 0
        for length in lengths:
            cuts.append(list(tied[at : at + length]))
            at += length
        assert at == len(tied)
        return cuts

    def core_two(pieces):
        return pieces + [flip(v, "ctx", 1, n_ctx) for v in pieces]

    def ctx_two(values):
        pieces = [values]
        for bit in far_bits:
            pieces = pieces + [flip(v, "ctx", bit, n_ctx) for v in pieces]
        return pieces

    def swap(values, axis):
        size = values.shape[axis] // 2
        keep = lax.dynamic_slice_in_dim(values, high * size, size, axis=axis)
        give = lax.dynamic_slice_in_dim(values, (1 - high) * size, size, axis=axis)
        return keep, give

    heads = w_query.shape[1] // n_ctx
    units = w_gate.shape[1] // n_ctx // 2

    def attn_slice(weight, axis):
        return lax.dynamic_slice_in_dim(weight, c * heads, heads, axis=axis)

    def wide_slice(weight, side, axis):
        return lax.dynamic_slice_in_dim(weight, (2 * c + side) * units, units, axis=axis)

    attn_pack = [attn_slice(w, 1) for w in (w_query, w_key, w_value)] + [attn_slice(w_out, 0).T]
    attn_full = lax.all_gather(jnp.concatenate(attn_pack, axis=1), "shard", axis=0, tiled=True)
    gains = lax.all_gather(jnp.stack([gain1, gain2]), "shard", axis=1, tiled=True).astype(F32)
    gain1_full, gain2_full = gains[0], gains[1]
    x = own_first(tokens[0]).astype(F32)
    unit1, factor1 = norm_forward(x)
    n1 = gather((unit1 * gain1_full).astype(BF), "ctx", n_ctx)
    x, unit1, factor1 = x[:short], unit1[:short], factor1[:short]
    seed_all = own_first(cotangent[0])
    seed = seed_all[:short]
    seed_all = folded(seed_all)
    dy_pair = ctx_ask(seed_all)

    def ordered(own, come, axis):
        return jnp.where(
            high == 0,
            jnp.concatenate([own, come], axis=axis),
            jnp.concatenate([come, own], axis=axis),
        )

    give_gate, give_up = wide_slice(w_gate, 1 - high, 1), wide_slice(w_up, 1 - high, 1)
    give_down = wide_slice(w_down, 1 - high, 0)
    own_gate, own_up, own_down = wide_slice(w_gate, high, 1), wide_slice(w_up, high, 1), wide_slice(w_down, high, 0)
    dy_far = pair(seed_all[:short])
    attn_full, n1, dy_far, give_gate, give_up, give_down, *dy_near = tie(
        attn_full, n1, dy_far, give_gate, give_up, give_down, *dy_pair
    )

    qkv_full, out_full = attn_full[:, : 3 * heads], attn_full[:, 3 * heads :]
    come_gate = pair(give_gate)
    dy_far = last_ask(*first_ask(dy_far))
    qkv = mm(n1, qkv_full)
    query = rotate(qkv[:, :heads], cosine, sine).astype(BF)
    key = rotate(qkv[:, heads : 2 * heads], cosine, sine).astype(BF)
    value = qkv[:, 2 * heads :].astype(BF)
    mixed = attend_forward(query, key, value, bias)
    mixed, come_gate, give_up, give_down, *rest = tie(mixed, come_gate, give_up, give_down, *dy_far, *dy_near)
    dy_far, dy_near = rest[:4], rest[4:]
    come_up = pair(give_up)
    gate_blocks = low_ask(ordered(own_gate, come_gate, 0))
    partial = core_give(mm_nt(mixed, out_full).astype(BF))
    partial = first_give(added(*partial))
    partial = last_give(*tie(*partial))
    come_up, give_down, n1, *rest = tie(come_up, give_down, n1, *partial, *gate_blocks)
    partial, gate_blocks = rest[:4], rest[4:]
    up_blocks = low_ask(ordered(own_up, come_up, 0))
    h1 = x + reduced(*partial).astype(F32)
    unit2, factor2 = norm_forward(h1)
    n2_short = folded((unit2 * gain2_full).astype(BF))
    n2_far = pair(n2_short)
    near = first_ask(n2_short)
    *near, gate_full = tie(*near, stacked(*gate_blocks))
    near = last_ask(*near)
    n1_folded = folded(n1)
    dy_near = stacked(*dy_near)
    n2_far, give_down, n1_folded, gate_full, dy_near, *rest = tie(
        n2_far, give_down, n1_folded, gate_full, dy_near, *near, *up_blocks, *dy_far
    )
    near, up_blocks, dy_far = rest[:4], rest[4:-4], rest[-4:]

    come_down = pair(give_down)
    far = first_ask(n2_far)
    near = core_ask(joined(*near))
    up_full = stacked(*up_blocks)
    up_full, *rest = tie(up_full, *near, *far)
    near, far = rest[:2], rest[2:]
    wide_full = jnp.concatenate([gate_full, up_full], axis=1)
    n2_near = stacked(*near)

    def wide_forward(n2):
        both = mm(n2, wide_full)
        gate, up = both[:, :units], both[:, units:]
        sigma = jax.nn.sigmoid(gate)
        silu = gate * sigma
        return (silu * up).astype(BF), silu, up * (sigma * (1.0 + gate * (1.0 - sigma)))

    def wide_backward(dy, silu, slope):
        grad_hidden = mm_nt(dy, down_full)
        return (grad_hidden * slope).astype(BF), (grad_hidden * silu).astype(BF)

    def wide_input(grad_gate, grad_up):
        return mm_nt(jnp.concatenate([grad_gate, grad_up], axis=1), wide_full).astype(BF)

    far = last_ask(*far)
    forward_near = wide_forward(n2_near)
    come_down, n2_near, *rest = tie(come_down, n2_near, *forward_near, *far, *dy_far)
    forward_near, far, dy_far = rest[:3], rest[3:7], rest[7:]
    down_blocks = low_ask(ordered(own_down, come_down, 1))
    far = core_ask(joined(*far))
    dy_near = core_ask(dy_near)
    dy_far = core_ask(joined(*dy_far))
    *far, dy_one, dy_two, one, two = tie(*far, *dy_near, *dy_far)
    dy_near = stacked(dy_one, dy_two)
    dy_far = [one, two]
    n2_far = stacked(*far)
    forward_far = wide_forward(n2_far)
    n2_far, dy_near, *rest = tie(n2_far, dy_near, *forward_far, *dy_far, *down_blocks)
    forward_far, dy_far, down_full = rest[:3], rest[3:5], jnp.concatenate(rest[5:], axis=1)
    gate_near, up_near = wide_backward(dy_near, *forward_near[1:])
    near = wide_input(gate_near, up_near)
    near, gate_near, dy_near, n2_near, *dy_far = tie(near, gate_near, dy_near, n2_near, *dy_far)
    near = core_give(near)
    dy_far = stacked(*dy_far)
    gate_far, up_far = wide_backward(dy_far, *forward_far[1:])
    gate_far, up_far, dy_far, dy_near, n2_near, *near = tie(gate_far, up_far, dy_far, dy_near, n2_near, *near)
    near = first_give(added(*near))
    far = wide_input(gate_far, up_far)
    far, dy_far, dy_near, n2_far, n2_near, *near = tie(far, dy_far, dy_near, n2_far, n2_near, *near)
    far = core_give(far)
    near = last_give(*near)
    hidden_near, hidden_far = forward_near[0], forward_far[0]
    grad_down = mm_t(stacked(hidden_near, hidden_far), stacked(dy_near, dy_far)).astype(BF)
    grad_down, gate_near, hidden_near, n2_near, *rest = tie(grad_down, gate_near, hidden_near, n2_near, *far, *near)
    far, near = packed(rest, 2, 4)
    near = reduced(*near)
    far = first_give(added(*far))
    down_low = low_give(grad_down, 1)
    near, gate_near, hidden_near, n2_far, n2_near, *far = tie(near, gate_near, hidden_near, n2_far, n2_near, *far)
    far = last_give(*far)
    n2_both = stacked(n2_near, n2_far)
    n2_both, up_near, gate_near, hidden_near, *rest = tie(n2_both, up_near, gate_near, hidden_near, *far, *down_low)
    far, down_low = packed(rest, 4, 2)

    far = pair(reduced(*far))
    down_keep, down_give = swap(added(*down_low), 1)
    down_keep = ctx_two(down_keep)
    grad_gate_w = mm_t(n2_both, stacked(gate_near, gate_far)).astype(BF)
    middle = n1.shape[0] // 2
    result_keep, result_give = [
        mm(stacked(hidden_near[part], hidden_far[part]), down_full).astype(BF)
        for part in (slice(None, middle), slice(middle, None))
    ]
    far, grad_gate_w, up_near, n2_both, down_give, result_keep, result_give, *down_keep = tie(
        far, grad_gate_w, up_near, n2_both, down_give, result_keep, result_give, *down_keep
    )
    gate_low = low_give(grad_gate_w, 0)
    down_come = pair(down_give)
    grad_n2 = unfolded(near.astype(F32) + far.astype(F32))
    back2, grad_norm2 = norm_backward(unit2, factor2, gain2_full, grad_n2)
    grad_h1 = seed.astype(F32) + back2
    dh1 = last_ask(*first_ask(grad_h1.astype(BF)))
    grad_up_w = mm_t(n2_both, stacked(up_near, up_far)).astype(BF)
    result = added(result_keep, flip(result_give, "ctx", 1, n_ctx))
    grad_up_w, result, down_come, *rest = tie(grad_up_w, result, down_come, *dh1, *gate_low)
    dh1, gate_low = packed(rest, 4, 2)

    dh1_own = joined(*dh1)
    dh1_come = flip(dh1_own, "ctx", 1, n_ctx)
    up_low = low_give(grad_up_w, 0)
    down_keep = core_two(down_keep)
    mixed_own, out_own = mm(dh1_own, out_full).astype(BF), mm_t(mixed[:middle], dh1_own)
    result, dh1_come, mixed_own, out_own, *rest = tie(result, dh1_come, mixed_own, out_own, *gate_low, *down_keep)
    gate_low, down_keep = packed(rest, 2, 2 * chips)
    result = first_give(result[:middle], result[middle:])
    grad_out = (out_own + mm_t(mixed[middle:], dh1_come)).astype(BF)
    share_out = lax.psum_scatter(grad_out, "shard", scatter_dimension=1, tiled=True)
    dh1_come, grad_out = tie(dh1_come, grad_out)
    gate_keep, gate_give = swap(added(*gate_low), 0)
    grad_mixed = stacked(mixed_own, mm(dh1_come, out_full).astype(BF))
    gate_come = pair(gate_give)
    gate_keep = ctx_two(gate_keep)
    dq, dk, dv = attend_backward(query, key, value, grad_mixed, bias, back_cosine, back_sine)
    dq, dk, dv, gate_come, down_come, *rest = tie(dq, dk, dv, gate_come, down_come, *result, *gate_keep, *up_low)
    result, gate_keep, up_low = packed(rest, 4, chips, 2)
    dqkv = jnp.concatenate([dq, dk, dv], axis=1)
    grad_qkv = mm_t(n1_folded, dqkv).astype(BF)

    dqkv, grad_qkv, gate_come, down_come, share_out, *rest = tie(
        dqkv, grad_qkv, gate_come, down_come, share_out, *result, *up_low, *gate_keep
    )
    result, up_low, gate_keep = packed(rest, 4, 2, chips)
    share_qkv = low_give(grad_qkv, 0)
    grad_n1 = core_give(mm_nt(dqkv, qkv_full).astype(BF))
    up_keep, up_give = swap(added(*up_low), 0)
    up_come = pair(up_give)
    result = last_give(*result)
    three = jnp.stack([gate_come, down_come, up_keep])
    three, *rest = tie(three, *grad_n1, *result, *gate_keep)
    grad_n1, result, gate_keep = packed(rest, 2, 4, chips)
    three, gate_keep = ctx_two(three), core_two(gate_keep)
    grad_n1 = added(*grad_n1)
    result_near, result_far = added(*result[:2]), pair(added(*result[2:]))
    up_come, grad_n1, result_near, result_far, *rest = tie(
        up_come, grad_n1, result_near, result_far, *share_qkv, *three, *gate_keep, *ctx_two(share_out)
    )
    share_qkv, three, gate_keep, share_out = packed(rest, 2, chips, 2 * chips, chips)
    share_qkv, qkv_give = swap(added(*share_qkv), 0)
    qkv_come = pair(qkv_give)
    grad_n1 = first_give(grad_n1)
    three = core_two(three)
    output = (h1 + unfolded(result_near.astype(F32) + result_far.astype(F32))).astype(BF)
    up_come, output, *rest = tie(up_come, output, *grad_n1, *three)
    grad_n1, three = packed(rest, 4, 2 * chips)
    grad_n1 = last_give(*grad_n1)
    up_come, output = ctx_two(up_come), tp_ask(output, 0)
    (grad_g,) = place(
        [(v[None], 0) for v in gate_keep] + [(v, 0) for v in three], both_halves, 2 * n_ctx, 1, 1
    )
    (grad_d,) = place(
        [(v[None], 0) for v in down_keep] + [(v, 1) for v in three], both_halves, 2 * n_ctx, 1, 0
    )
    qkv_come, share_qkv, grad_g, grad_d, *rest = tie(
        qkv_come, share_qkv, grad_g, grad_d, *grad_n1, *up_come, *output
    )
    grad_n1, up_come, output = packed(rest, 4, chips, 2)
    share_qkv = ctx_two(added(share_qkv, qkv_come))
    back1, grad_norm1 = norm_backward(unit1, factor1, gain1_full, reduced(*grad_n1).astype(F32))
    input_grad, output = tp_ask((grad_h1 + back1).astype(BF), 0), as_placed(stacked(*output))
    norms = jnp.stack([grad_norm1, grad_norm2]).reshape(-1, 128)

    def met(values, axis, bits, size):
        for bit in bits:
            values = values + flip(values, axis, bit, size)
        return values

    norms, up_come = met(norms, "tp", tp_bits, n_tp), core_two(up_come)
    norms, output, *rest = tie(norms, output, *share_qkv, *input_grad, *up_come)
    share_qkv, input_grad, up_come = packed(rest, chips, 2, 2 * chips)
    norms, share_qkv, share_out = met(norms, "ctx", [1], n_ctx), core_two(share_qkv), core_two(share_out)
    input_grad = as_placed(stacked(*input_grad))
    (grad_u,) = place([(v, 2) for v in three] + [(v[None], 0) for v in up_come], both_halves, 2 * n_ctx, 1, 1)
    grad_u, norms, *rest = tie(grad_u, norms, *share_qkv, *share_out)
    share_qkv, share_out = packed(rest, 2 * chips, 2 * chips)
    norms = met(norms, "ctx", far_bits, n_ctx)
    (grad_o,) = place([(v[None], 0) for v in share_out], owners, n_ctx, 1, 0)
    grad_o, norms, *share_qkv = tie(grad_o, norms, *share_qkv)
    norms = met(norms, "shard", low_bits, n_shard)
    grad_q, grad_k, grad_v = place([(v[None], 0) for v in share_qkv], owners, n_ctx, 3, 1)
    grad_q, grad_k, grad_v, norms = tie(grad_q, grad_k, grad_v, norms)
    norms = met(norms, "shard", [top], n_shard)
    norms = lax.dynamic_slice_in_dim(norms.reshape(2, width), z * block, block, axis=1)
    return (output, input_grad, norms[0], grad_q, grad_k, grad_v, grad_o, norms[1], grad_g, grad_u, grad_d)


def solution(mesh):
    n_shard, n_ctx, n_tp = mesh.shape["shard"], mesh.shape["ctx"], mesh.shape["tp"]

    def local(*arguments):
        return body(n_shard, n_ctx, n_tp, *arguments)

    return jax.shard_map(
        local,
        mesh=mesh,
        in_specs=(
            P("shard", "ctx", None),
            P("shard", None),
            P("shard"),
            P("shard", "tp"),
            P("shard", "tp"),
            P("shard", "tp"),
            P("tp", "shard"),
            P("shard"),
            P("shard", "tp"),
            P("shard", "tp"),
            P("tp", "shard"),
            P("shard", "ctx", None),
        ),
        out_specs=(
            P("shard", "ctx", None),
            P("shard", "ctx", None),
            P("shard"),
            P("shard", "tp"),
            P("shard", "tp"),
            P("shard", "tp"),
            P("tp", "shard"),
            P("shard"),
            P("shard", "tp"),
            P("shard", "tp"),
            P("tp", "shard"),
        ),
        check_vma=False,
    )
```

```python
import math

import jax
import jax.numpy as jnp
from jax import lax
from jax.experimental import pallas as pl
from jax.experimental.pallas import tpu as pltpu
from jax.sharding import PartitionSpec as P

HD = 64
PIECE = 256

EPS = 1e-05
ROPE_BASE = 130000.0
BF = jnp.bfloat16
F32 = jnp.float32


def flip(values, axis, bit, size):
    return lax.ppermute(values, axis, [(i, i ^ bit) for i in range(size)])


def bits_of(size):
    found, bit = [], size // 2
    while bit >= 1:
        found.append(bit)
        bit //= 2
    return found


def order_of(size):
    order = [0]
    for bit in bits_of(size):
        order = order + [o | bit for o in order]
    return order


def tie(*values):
    return lax.optimization_barrier(values)


def gather(block, axis, size, dim=0):
    for bit in bits_of(size):
        block = jnp.concatenate([block, flip(block, axis, bit, size)], axis=dim)
    return block


def reduce_step(partial, axis, bit, size, dim=0):
    keep, give = jnp.split(partial, 2, axis=dim)
    come = flip(give, axis, bit, size)
    return (keep.astype(F32) + come.astype(F32)).astype(BF)


def mm(left, right):
    return jnp.dot(left, right, preferred_element_type=F32)


def mm_t(left, right):
    return lax.dot_general(left, right, (((0,), (0,)), ((), ())), preferred_element_type=F32)


def mm_nt(left, right):
    return lax.dot_general(left, right, (((1,), (1,)), ((), ())), preferred_element_type=F32)


def rope_tables(positions):
    frequency = jnp.power(ROPE_BASE, -2.0 * jnp.arange(HD // 2, dtype=F32) / HD)
    angles = positions.astype(F32)[:, None] * frequency[None, :]
    return jnp.cos(angles)[:, None, :], jnp.sin(angles)[:, None, :]


def rotate(values, cosine, sine):
    rows, columns = values.shape
    halves = values.reshape(rows, columns // HD, 2, HD // 2)
    front, back = halves[:, :, 0, :], halves[:, :, 1, :]
    turned = jnp.stack([front * cosine - back * sine, back * cosine + front * sine], axis=2)
    return turned.reshape(rows, columns)


def visible(begins, places):
    inside = (places[None, :] >= begins[:, None]) & (places[None, :] < begins[:, None] + PIECE)
    shared = jnp.any(inside[:, :, None] & inside[:, None, :], axis=0)
    return (places[None, :] <= places[:, None]) | shared


def attention_scores(query, key, bias):
    return mm_nt(query * jnp.asarray(1.0 / math.sqrt(HD), BF), key) + bias


def pair_specs(rows, count):
    return [pl.BlockSpec((rows, 2 * HD), lambda i: (0, i)) for _ in range(count)]


def attend_forward(query, key, value, bias):
    rows, columns = query.shape
    block = min(256, rows)

    def kernel(query_ref, key_ref, value_ref, bias_ref, out_ref, totals_ref):
        for head in range(2):
            lanes = slice(head * HD, (head + 1) * HD)
            k, v = key_ref[:, lanes], value_ref[:, lanes]
            for start in range(0, rows, block):
                now = slice(start, start + block)
                scores = attention_scores(query_ref[now, lanes], k, bias_ref[now, :])
                top = jnp.max(scores, axis=-1, keepdims=True)
                powers = jnp.exp(scores - top)
                total = jnp.sum(powers, axis=-1, keepdims=True)
                out_ref[now, lanes] = (mm(powers.astype(BF), v) * (1.0 / total)).astype(BF)
                totals_ref[now, lanes] = jnp.broadcast_to(top + jnp.log(total), (block, HD))

    return pl.pallas_call(
        kernel,
        grid=(columns // (2 * HD),),
        in_specs=pair_specs(rows, 3) + [pl.BlockSpec((rows, rows), lambda i: (0, 0))],
        out_specs=pair_specs(rows, 2),
        out_shape=[jax.ShapeDtypeStruct((rows, columns), BF), jax.ShapeDtypeStruct((rows, columns), F32)],
        compiler_params=pltpu.CompilerParams(vmem_limit_bytes=40 * 1024 * 1024),
        cost_estimate=pl.CostEstimate(
            flops=16 * rows * rows * columns,
            transcendentals=rows * rows * columns // HD,
            bytes_accessed=8 * rows * columns + 4 * rows * rows,
        ),
    )(query, key, value, bias)


def attend_backward(query, key, value, totals, grad, bias, cosine, sine):
    rows, columns = query.shape
    block = min(256, rows)
    scale = 1.0 / math.sqrt(HD)

    def kernel(query_ref, key_ref, value_ref, totals_ref, grad_ref, bias_ref, cos_ref, sin_ref, dq_ref, dk_ref, dv_ref, q_acc, k_acc):
        lane = lax.broadcasted_iota(jnp.int32, (rows, 2 * HD), 1)
        front = lane % HD < HD // 2

        def turned_back(values):
            other = jnp.where(front, pltpu.roll(values, 2 * HD - HD // 2, 1), pltpu.roll(values, HD // 2, 1))
            return (values * cos_ref[...] + other * sin_ref[...]).astype(BF)

        for head in range(2):
            lanes = slice(head * HD, (head + 1) * HD)
            k, v = key_ref[:, lanes], value_ref[:, lanes]
            k_sum = jnp.zeros((HD, rows), F32)
            v_sum = jnp.zeros((HD, rows), F32)
            for start in range(0, rows, block):
                now = slice(start, start + block)
                q, g = query_ref[now, lanes], grad_ref[now, lanes]
                total = totals_ref[now, head * HD : head * HD + 1]
                probs = jnp.exp(attention_scores(q, k, bias_ref[now, :]) - total)
                v_sum += mm_t(g, probs.astype(BF))
                grad_probs = mm_nt(g, v)
                centre = jnp.sum(probs * grad_probs, axis=-1, keepdims=True)
                grad_scores = (probs * (grad_probs - centre)).astype(BF)
                q_acc[now, lanes] = mm(grad_scores, k) * scale
                k_sum += mm_t(q, grad_scores)
            k_acc[:, lanes] = k_sum.T * scale
            dv_ref[:, lanes] = v_sum.T.astype(BF)
        dq_ref[...] = turned_back(q_acc[...])
        dk_ref[...] = turned_back(k_acc[...])

    return pl.pallas_call(
        kernel,
        grid=(columns // (2 * HD),),
        in_specs=pair_specs(rows, 5)
        + [pl.BlockSpec((rows, rows), lambda i: (0, 0))]
        + [pl.BlockSpec((rows, 2 * HD), lambda i: (0, 0))] * 2,
        out_specs=pair_specs(rows, 3),
        out_shape=[jax.ShapeDtypeStruct((rows, columns), BF)] * 3,
        scratch_shapes=[pltpu.VMEM((rows, 2 * HD), F32)] * 2,
        compiler_params=pltpu.CompilerParams(vmem_limit_bytes=48 * 1024 * 1024),
        cost_estimate=pl.CostEstimate(
            flops=30 * rows * rows * columns,
            transcendentals=rows * rows * columns // HD,
            bytes_accessed=14 * rows * columns + 4 * rows * rows,
        ),
    )(query, key, value, totals, grad, bias, cosine, sine)


def norm_forward(values):
    factor = lax.rsqrt(jnp.mean(values * values, axis=-1, keepdims=True) + EPS)
    return values * factor, factor


def norm_backward(unit, factor, gain, grad):
    scaled = grad * gain
    back = factor * (scaled - unit * jnp.mean(scaled * unit, axis=-1, keepdims=True))
    return back, jnp.sum(grad * unit, axis=0)


def place(pieces, targets, blocks, parts, axis):
    rows, columns = pieces[0][0].shape[1], pieces[0][0].shape[2] // parts
    total = len(pieces)

    def kernel(targets_ref, *refs):
        ins, outs = refs[:total], refs[total:]
        i = pl.program_id(0)
        for at, ref in enumerate(ins):

            @pl.when(i == at)
            def _():
                for j, out in enumerate(outs):
                    out[...] = ref[:, j * columns : (j + 1) * columns].astype(F32)

    def go(i, t):
        return (0, t[i]) if axis == 1 else (t[i], 0)

    shape = (rows, columns * blocks) if axis == 1 else (rows * blocks, columns)
    return pl.pallas_call(
        kernel,
        grid_spec=pltpu.PrefetchScalarGridSpec(
            num_scalar_prefetch=1,
            grid=(total,),
            in_specs=[
                pl.BlockSpec((None, rows, parts * columns), lambda i, t, at=at: (at, 0, 0)) for _, at in pieces
            ],
            out_specs=[pl.BlockSpec((rows, columns), go) for _ in range(parts)],
        ),
        out_shape=[jax.ShapeDtypeStruct(shape, F32) for _ in range(parts)],
        compiler_params=pltpu.CompilerParams(vmem_limit_bytes=32 * 1024 * 1024),
        cost_estimate=pl.CostEstimate(
            flops=0, transcendentals=0, bytes_accessed=6 * parts * rows * columns * blocks
        ),
    )(targets, *[array for array, _ in pieces])


def body(n_shard, n_ctx, n_tp, *arguments):
    (tokens, piece_starts, gain1, w_query, w_key, w_value, w_out, gain2, w_gate, w_up, w_down, cotangent) = arguments
    sequences, rows, width = tokens.shape
    assert sequences == 1
    z, c, t = lax.axis_index("shard"), lax.axis_index("ctx"), lax.axis_index("tp")
    short = rows // n_tp
    top = n_shard // 2
    high, low = z // top, z % top

    offsets = [(o, p) for o in order_of(n_ctx) for p in order_of(n_tp)]
    places = jnp.concatenate(
        [(c ^ o) * rows + (t ^ p) * short + jnp.arange(short, dtype=jnp.int32) for o, p in offsets]
    )
    bias = jnp.where(visible(piece_starts[0], places), 0.0, -1e30).astype(F32)
    cosine, sine = rope_tables(places)
    back_cosine = jnp.tile(cosine[:, 0, :], (1, 4))
    back_sine = jnp.tile(jnp.concatenate([sine[:, 0, :], -sine[:, 0, :]], axis=1), (1, 2))

    def own_first(values):
        return jnp.concatenate(
            [lax.dynamic_slice_in_dim(values, (t ^ p) * short, short, axis=0) for p in order_of(n_tp)]
        )

    def as_placed(found):
        result = jnp.zeros_like(found)
        for at, p in enumerate(order_of(n_tp)):
            block = found[at * short : (at + 1) * short]
            result = lax.dynamic_update_slice_in_dim(result, block, (t ^ p) * short, axis=0)
        return result[None]

    owners = jnp.stack([c ^ o for o in order_of(n_ctx)]).astype(jnp.int32)
    both_halves = jnp.concatenate([2 * owners + high, 2 * owners + 1 - high]).astype(jnp.int32)

    far_bits, tp_bits = bits_of(n_ctx)[:-1], bits_of(n_tp)
    chips = n_ctx // 2
    half = width // 2

    def halves(values, axis, bit, size, dim=0):
        keep, give = jnp.split(values, 2, axis=dim)
        return [keep, flip(give, axis, bit, size)]

    def added(keep, come):
        return (keep.astype(F32) + come.astype(F32)).astype(BF)

    def core_give(values):
        return halves(values, "ctx", 1, n_ctx)

    def ctx_give(values):
        for bit in reversed(far_bits[1:]):
            values = reduce_step(values, "ctx", bit, n_ctx)
        return halves(values, "ctx", far_bits[0], n_ctx)

    def tp_give(values, dim):
        for bit in reversed(tp_bits[1:]):
            values = reduce_step(values, "tp", bit, n_tp, dim)
        return halves(values, "tp", tp_bits[0], n_tp, dim)

    def first_give(left, right=None):
        if right is None:
            left, right = left[:, :half], left[:, half:]
        return ctx_give(left) + tp_give(right.reshape(chips, n_tp * short, right.shape[1]), 1)

    def last_give(keep, come, other_keep, other_come):
        right = added(other_keep, other_come).reshape(chips * short, keep.shape[1])
        return tp_give(added(keep, come), 0) + ctx_give(right)

    def reduced(keep, come, other_keep, other_come):
        return jnp.concatenate([added(keep, come), added(other_keep, other_come)], axis=1)

    def ctx_ask(values):
        for bit in far_bits[:-1]:
            values = jnp.concatenate([values, flip(values, "ctx", bit, n_ctx)], axis=0)
        return [values, flip(values, "ctx", far_bits[-1], n_ctx)]

    def tp_ask(values, dim):
        for bit in tp_bits[:-1]:
            values = jnp.concatenate([values, flip(values, "tp", bit, n_tp)], axis=dim)
        return [values, flip(values, "tp", tp_bits[-1], n_tp)]

    def first_ask(values):
        return tp_ask(values[:, :half], 0) + ctx_ask(values[:, half:])

    def last_ask(own, come, other_own, other_come):
        right = jnp.concatenate([other_own, other_come], axis=0).reshape(chips, short, half)
        return ctx_ask(jnp.concatenate([own, come], axis=0)) + tp_ask(right, 1)

    def joined(own, come, other_own, other_come):
        left = jnp.concatenate([own, come], axis=0)
        right = jnp.concatenate([other_own, other_come], axis=1).reshape(left.shape)
        return jnp.concatenate([left, right], axis=1)

    def core_ask(values):
        return [values, flip(values, "ctx", 1, n_ctx)]

    def stacked(*parts):
        return jnp.concatenate(parts, axis=0)

    def pair(values):
        return flip(values, "shard", top, n_shard)

    block = width // n_shard
    low_order = order_of(top)
    low_bits = bits_of(top)
    planes = [[side * top + o for o in range(top)] for side in range(2)]

    def low_sum(values, dim):
        where = jnp.asarray([low_order.index(o) for o in range(top)], jnp.int32)
        size = values.shape[dim] // top
        parts = [lax.dynamic_slice_in_dim(values, where[low ^ o] * size, size, axis=dim) for o in range(top)]
        return lax.psum_scatter(
            jnp.concatenate(parts, axis=dim), "shard", scatter_dimension=dim, tiled=True, axis_index_groups=planes
        )

    def folded(values):
        starts = [(side * top + (low ^ o)) * block for o in low_order for side in range(2)]
        return jnp.concatenate([lax.dynamic_slice_in_dim(values, s, block, axis=1) for s in starts], axis=1)

    def unfolded(values):
        where = jnp.asarray([low_order.index(o) for o in range(top)], jnp.int32)
        starts = [(2 * where[low ^ o] + side) * block for side in range(2) for o in range(top)]
        return jnp.concatenate([lax.dynamic_slice_in_dim(values, s, block, axis=1) for s in starts], axis=1)

    def low_ask(values):
        blocks = [values]
        for bit in low_bits:
            blocks = blocks + [flip(v, "shard", bit, n_shard) for v in blocks]
        return blocks

    def low_give(values, dim):
        for bit in reversed(low_bits[1:]):
            values = reduce_step(values, "shard", bit, n_shard, dim)
        return halves(values, "shard", low_bits[0], n_shard, dim)

    def packed(tied, *lengths):
        cuts, at = [], 0
        for length in lengths:
            cuts.append(list(tied[at : at + length]))
            at += length
        assert at == len(tied)
        return cuts

    def core_two(pieces):
        return pieces + [flip(v, "ctx", 1, n_ctx) for v in pieces]

    def ctx_two(values):
        pieces = [values]
        for bit in far_bits:
            pieces = pieces + [flip(v, "ctx", bit, n_ctx) for v in pieces]
        return pieces

    def swap(values, axis):
        size = values.shape[axis] // 2
        keep = lax.dynamic_slice_in_dim(values, high * size, size, axis=axis)
        give = lax.dynamic_slice_in_dim(values, (1 - high) * size, size, axis=axis)
        return keep, give

    heads = w_query.shape[1] // n_ctx
    units = w_gate.shape[1] // n_ctx // 2

    def attn_slice(weight, axis):
        return lax.dynamic_slice_in_dim(weight, c * heads, heads, axis=axis)

    def wide_slice(weight, side, axis):
        return lax.dynamic_slice_in_dim(weight, (2 * c + side) * units, units, axis=axis)

    attn_pack = [attn_slice(w, 1) for w in (w_query, w_key, w_value)] + [attn_slice(w_out, 0).T]
    attn_full = lax.all_gather(jnp.concatenate(attn_pack, axis=1), "shard", axis=0, tiled=True)
    gains = lax.all_gather(jnp.stack([gain1, gain2]), "shard", axis=1, tiled=True).astype(F32)
    gain1_full, gain2_full = gains[0], gains[1]
    x = own_first(tokens[0]).astype(F32)
    unit1, factor1 = norm_forward(x)
    n1 = gather((unit1 * gain1_full).astype(BF), "ctx", n_ctx)
    x, unit1, factor1 = x[:short], unit1[:short], factor1[:short]
    seed_all = own_first(cotangent[0])
    seed = seed_all[:short]
    seed_all = folded(seed_all)
    dy_pair = ctx_ask(seed_all)

    def ordered(own, come, axis):
        return jnp.where(
            high == 0,
            jnp.concatenate([own, come], axis=axis),
            jnp.concatenate([come, own], axis=axis),
        )

    give_gate, give_up = wide_slice(w_gate, 1 - high, 1), wide_slice(w_up, 1 - high, 1)
    give_down = wide_slice(w_down, 1 - high, 0)
    own_gate, own_up, own_down = wide_slice(w_gate, high, 1), wide_slice(w_up, high, 1), wide_slice(w_down, high, 0)
    dy_far = pair(seed_all[:short])
    attn_full, n1, dy_far, give_gate, give_up, give_down, *dy_near = tie(
        attn_full, n1, dy_far, give_gate, give_up, give_down, *dy_pair
    )

    qkv_full, out_full = attn_full[:, : 3 * heads], attn_full[:, 3 * heads :]
    come_gate = pair(give_gate)
    dy_far = last_ask(*first_ask(dy_far))
    qkv = mm(n1, qkv_full)
    query = rotate(qkv[:, :heads], cosine, sine).astype(BF)
    key = rotate(qkv[:, heads : 2 * heads], cosine, sine).astype(BF)
    value = qkv[:, 2 * heads :].astype(BF)
    mixed, totals = attend_forward(query, key, value, bias)
    mixed, come_gate, give_up, give_down, *rest = tie(mixed, come_gate, give_up, give_down, *dy_far, *dy_near)
    dy_far, dy_near = rest[:4], rest[4:]
    come_up = pair(give_up)
    gate_blocks = low_ask(ordered(own_gate, come_gate, 0))
    partial = core_give(mm_nt(mixed, out_full).astype(BF))
    partial = first_give(added(*partial))
    partial = last_give(*tie(*partial))
    come_up, give_down, n1, *rest = tie(come_up, give_down, n1, *partial, *gate_blocks)
    partial, gate_blocks = rest[:4], rest[4:]
    up_blocks = low_ask(ordered(own_up, come_up, 0))
    h1 = x + reduced(*partial).astype(F32)
    unit2, factor2 = norm_forward(h1)
    n2_short = folded((unit2 * gain2_full).astype(BF))
    n2_far = pair(n2_short)
    near = first_ask(n2_short)
    *near, gate_full = tie(*near, stacked(*gate_blocks))
    near = last_ask(*near)
    n1_folded = folded(n1)
    dy_near = stacked(*dy_near)
    n2_far, give_down, n1_folded, gate_full, dy_near, *rest = tie(
        n2_far, give_down, n1_folded, gate_full, dy_near, *near, *up_blocks, *dy_far
    )
    near, up_blocks, dy_far = rest[:4], rest[4:-4], rest[-4:]

    come_down = pair(give_down)
    far = first_ask(n2_far)
    near = core_ask(joined(*near))
    up_full = stacked(*up_blocks)
    up_full, *rest = tie(up_full, *near, *far)
    near, far = rest[:2], rest[2:]
    wide_full = jnp.concatenate([gate_full, up_full], axis=1)
    n2_near = stacked(*near)

    def wide_forward(n2):
        both = mm(n2, wide_full)
        gate, up = both[:, :units], both[:, units:]
        sigma = jax.nn.sigmoid(gate)
        silu = gate * sigma
        return (silu * up).astype(BF), silu, up * (sigma * (1.0 + gate * (1.0 - sigma)))

    def wide_backward(dy, silu, slope):
        grad_hidden = mm_nt(dy, down_full)
        return (grad_hidden * slope).astype(BF), (grad_hidden * silu).astype(BF)

    def wide_input(grad_gate, grad_up):
        return mm_nt(jnp.concatenate([grad_gate, grad_up], axis=1), wide_full).astype(BF)

    far = last_ask(*far)
    forward_near = wide_forward(n2_near)
    come_down, n2_near, *rest = tie(come_down, n2_near, *forward_near, *far, *dy_far)
    forward_near, far, dy_far = rest[:3], rest[3:7], rest[7:]
    down_blocks = low_ask(ordered(own_down, come_down, 1))
    far = core_ask(joined(*far))
    dy_near = core_ask(dy_near)
    dy_far = core_ask(joined(*dy_far))
    *far, dy_one, dy_two, one, two = tie(*far, *dy_near, *dy_far)
    dy_near = stacked(dy_one, dy_two)
    dy_far = [one, two]
    n2_far = stacked(*far)
    forward_far = wide_forward(n2_far)
    down_part = mm_t(forward_near[0], dy_near)
    n2_far, dy_near, down_part, *rest = tie(n2_far, dy_near, down_part, *forward_far, *dy_far, *down_blocks)
    forward_far, dy_far, down_full = rest[:3], rest[3:5], jnp.concatenate(rest[5:], axis=1)
    gate_near, up_near = wide_backward(dy_near, *forward_near[1:])
    near = wide_input(gate_near, up_near)
    near, gate_near, n2_near, *dy_far = tie(near, gate_near, n2_near, *dy_far)
    near = core_give(near)
    dy_far = stacked(*dy_far)
    gate_far, up_far = wide_backward(dy_far, *forward_far[1:])
    gate_far, up_far, dy_far, n2_near, *near = tie(gate_far, up_far, dy_far, n2_near, *near)
    near = first_give(added(*near))
    hidden_near, hidden_far = forward_near[0], forward_far[0]
    grad_down = (down_part + mm_t(hidden_far, dy_far)).astype(BF)
    down_low = low_sum(grad_down, 1)
    far = wide_input(gate_far, up_far)
    far, grad_down, n2_far, n2_near, *near = tie(far, grad_down, n2_far, n2_near, *near)
    far = core_give(far)
    near = last_give(*near)
    gate_near, hidden_near, n2_near, down_low, *rest = tie(gate_near, hidden_near, n2_near, down_low, *far, *near)
    far, near = packed(rest, 2, 4)
    near = reduced(*near)
    far = first_give(added(*far))
    down_keep, down_give = swap(down_low, 1)
    down_come = pair(down_give)
    near, gate_near, hidden_near, n2_far, n2_near, *far = tie(near, gate_near, hidden_near, n2_far, n2_near, *far)
    far = last_give(*far)
    n2_both = stacked(n2_near, n2_far)
    n2_both, up_near, gate_near, hidden_near, down_keep, down_come, *far = tie(
        n2_both, up_near, gate_near, hidden_near, down_keep, down_come, *far
    )

    far = pair(reduced(*far))
    down_keep = ctx_two(down_keep)
    grad_gate_w = mm_t(n2_both, stacked(gate_near, gate_far)).astype(BF)
    middle = n1.shape[0] // 2
    result_keep, result_give = [
        mm(stacked(hidden_near[part], hidden_far[part]), down_full).astype(BF)
        for part in (slice(None, middle), slice(middle, None))
    ]
    far, grad_gate_w, up_near, n2_both, result_keep, result_give, *down_keep = tie(
        far, grad_gate_w, up_near, n2_both, result_keep, result_give, *down_keep
    )
    gate_low = low_give(grad_gate_w, 0)
    grad_n2 = unfolded(near.astype(F32) + far.astype(F32))
    back2, grad_norm2 = norm_backward(unit2, factor2, gain2_full, grad_n2)
    grad_h1 = seed.astype(F32) + back2
    dh1 = last_ask(*first_ask(grad_h1.astype(BF)))
    grad_up_w = mm_t(n2_both, stacked(up_near, up_far)).astype(BF)
    result = added(result_keep, flip(result_give, "ctx", 1, n_ctx))
    grad_up_w, result, *rest = tie(grad_up_w, result, *dh1, *gate_low)
    dh1, gate_low = packed(rest, 4, 2)

    dh1_own = joined(*dh1)
    dh1_come = flip(dh1_own, "ctx", 1, n_ctx)
    up_low = low_give(grad_up_w, 0)
    down_keep = core_two(down_keep)
    mixed_own, out_own = mm(dh1_own, out_full).astype(BF), mm_t(mixed[:middle], dh1_own)
    result, dh1_come, mixed_own, out_own, *rest = tie(result, dh1_come, mixed_own, out_own, *gate_low, *down_keep)
    gate_low, down_keep = packed(rest, 2, 2 * chips)
    result = first_give(result[:middle], result[middle:])
    grad_out = (out_own + mm_t(mixed[middle:], dh1_come)).astype(BF)
    share_out = lax.psum_scatter(grad_out, "shard", scatter_dimension=1, tiled=True)
    dh1_come, grad_out = tie(dh1_come, grad_out)
    gate_keep, gate_give = swap(added(*gate_low), 0)
    grad_mixed = stacked(mixed_own, mm(dh1_come, out_full).astype(BF))
    gate_come = pair(gate_give)
    gate_keep = ctx_two(gate_keep)
    dq, dk, dv = attend_backward(query, key, value, totals, grad_mixed, bias, back_cosine, back_sine)
    dq, dk, dv, gate_come, down_come, *rest = tie(dq, dk, dv, gate_come, down_come, *result, *gate_keep, *up_low)
    result, gate_keep, up_low = packed(rest, 4, chips, 2)
    dqkv = jnp.concatenate([dq, dk, dv], axis=1)
    grad_qkv = mm_t(n1_folded, dqkv).astype(BF)

    dqkv, grad_qkv, gate_come, down_come, share_out, *rest = tie(
        dqkv, grad_qkv, gate_come, down_come, share_out, *result, *up_low, *gate_keep
    )
    result, up_low, gate_keep = packed(rest, 4, 2, chips)
    share_qkv = low_give(grad_qkv, 0)
    grad_n1 = core_give(mm_nt(dqkv, qkv_full).astype(BF))
    up_keep, up_give = swap(added(*up_low), 0)
    up_come = pair(up_give)
    result = last_give(*result)
    three = jnp.stack([gate_come, down_come, up_keep])
    three, *rest = tie(three, *grad_n1, *result, *gate_keep)
    grad_n1, result, gate_keep = packed(rest, 2, 4, chips)
    three, gate_keep = ctx_two(three), core_two(gate_keep)
    grad_n1 = added(*grad_n1)
    result_near, result_far = added(*result[:2]), pair(added(*result[2:]))
    up_come, grad_n1, result_near, result_far, *rest = tie(
        up_come, grad_n1, result_near, result_far, *share_qkv, *three, *gate_keep, *ctx_two(share_out)
    )
    share_qkv, three, gate_keep, share_out = packed(rest, 2, chips, 2 * chips, chips)
    share_qkv, qkv_give = swap(added(*share_qkv), 0)
    qkv_come = pair(qkv_give)
    grad_n1 = first_give(grad_n1)
    three = core_two(three)
    output = (h1 + unfolded(result_near.astype(F32) + result_far.astype(F32))).astype(BF)
    up_come, output, *rest = tie(up_come, output, *grad_n1, *three)
    grad_n1, three = packed(rest, 4, 2 * chips)
    grad_n1 = last_give(*grad_n1)
    up_come, output = ctx_two(up_come), tp_ask(output, 0)
    (grad_g,) = place(
        [(v[None], 0) for v in gate_keep] + [(v, 0) for v in three], both_halves, 2 * n_ctx, 1, 1
    )
    (grad_d,) = place(
        [(v[None], 0) for v in down_keep] + [(v, 1) for v in three], both_halves, 2 * n_ctx, 1, 0
    )
    qkv_come, share_qkv, grad_g, grad_d, *rest = tie(
        qkv_come, share_qkv, grad_g, grad_d, *grad_n1, *up_come, *output
    )
    grad_n1, up_come, output = packed(rest, 4, chips, 2)
    share_qkv = ctx_two(added(share_qkv, qkv_come))
    back1, grad_norm1 = norm_backward(unit1, factor1, gain1_full, reduced(*grad_n1).astype(F32))
    input_grad, output = tp_ask((grad_h1 + back1).astype(BF), 0), as_placed(stacked(*output))
    norms = jnp.stack([grad_norm1, grad_norm2]).reshape(-1, 128)

    def met(values, axis, bits, size):
        for bit in bits:
            values = values + flip(values, axis, bit, size)
        return values

    norms, up_come = met(norms, "tp", tp_bits, n_tp), core_two(up_come)
    norms, output, *rest = tie(norms, output, *share_qkv, *input_grad, *up_come)
    share_qkv, input_grad, up_come = packed(rest, chips, 2, 2 * chips)
    norms, share_qkv, share_out = met(norms, "ctx", [1], n_ctx), core_two(share_qkv), core_two(share_out)
    norms, *rest = tie(norms, *share_qkv, *share_out)
    share_qkv, share_out = packed(rest, 2 * chips, 2 * chips)
    norms = met(norms, "ctx", far_bits, n_ctx)
    input_grad = as_placed(stacked(*input_grad))
    grad_q, grad_k, grad_v = place([(v[None], 0) for v in share_qkv], owners, n_ctx, 3, 1)
    grad_q, grad_k, grad_v, norms = tie(grad_q, grad_k, grad_v, norms)
    norms = met(norms, "shard", low_bits, n_shard)
    (grad_u,) = place([(v, 2) for v in three] + [(v[None], 0) for v in up_come], both_halves, 2 * n_ctx, 1, 1)
    grad_u, norms = tie(grad_u, norms)
    norms = met(norms, "shard", [top], n_shard)
    (grad_o,) = place([(v[None], 0) for v in share_out], owners, n_ctx, 1, 0)
    norms = lax.dynamic_slice_in_dim(norms.reshape(2, width), z * block, block, axis=1)
    return (output, input_grad, norms[0], grad_q, grad_k, grad_v, grad_o, norms[1], grad_g, grad_u, grad_d)


def solution(mesh):
    n_shard, n_ctx, n_tp = mesh.shape["shard"], mesh.shape["ctx"], mesh.shape["tp"]

    def local(*arguments):
        return body(n_shard, n_ctx, n_tp, *arguments)

    return jax.shard_map(
        local,
        mesh=mesh,
        in_specs=(
            P("shard", "ctx", None),
            P("shard", None),
            P("shard"),
            P("shard", "tp"),
            P("shard", "tp"),
            P("shard", "tp"),
            P("tp", "shard"),
            P("shard"),
            P("shard", "tp"),
            P("shard", "tp"),
            P("tp", "shard"),
            P("shard", "ctx", None),
        ),
        out_specs=(
            P("shard", "ctx", None),
            P("shard", "ctx", None),
            P("shard"),
            P("shard", "tp"),
            P("shard", "tp"),
            P("shard", "tp"),
            P("tp", "shard"),
            P("shard"),
            P("shard", "tp"),
            P("shard", "tp"),
            P("tp", "shard"),
        ),
        check_vma=False,
    )
```

```python
import math

import jax
import jax.numpy as jnp
from jax import lax
from jax.experimental import pallas as pl
from jax.experimental.pallas import tpu as pltpu
from jax.sharding import PartitionSpec as P

HD = 64
PIECE = 256

EPS = 1e-05
ROPE_BASE = 130000.0
BF = jnp.bfloat16
F32 = jnp.float32


def flip(values, axis, bit, size):
    return lax.ppermute(values, axis, [(i, i ^ bit) for i in range(size)])


def bits_of(size):
    found, bit = [], size // 2
    while bit >= 1:
        found.append(bit)
        bit //= 2
    return found


def order_of(size):
    order = [0]
    for bit in bits_of(size):
        order = order + [o | bit for o in order]
    return order


def tie(*values):
    return lax.optimization_barrier(values)


def gather(block, axis, size, dim=0):
    for bit in bits_of(size):
        block = jnp.concatenate([block, flip(block, axis, bit, size)], axis=dim)
    return block


def reduce_step(partial, axis, bit, size, dim=0):
    keep, give = jnp.split(partial, 2, axis=dim)
    come = flip(give, axis, bit, size)
    return (keep.astype(F32) + come.astype(F32)).astype(BF)


def mm(left, right):
    return jnp.dot(left, right, preferred_element_type=F32)


def mm_t(left, right):
    return lax.dot_general(left, right, (((0,), (0,)), ((), ())), preferred_element_type=F32)


def mm_nt(left, right):
    return lax.dot_general(left, right, (((1,), (1,)), ((), ())), preferred_element_type=F32)


def rope_tables(positions):
    frequency = jnp.power(ROPE_BASE, -2.0 * jnp.arange(HD // 2, dtype=F32) / HD)
    angles = positions.astype(F32)[:, None] * frequency[None, :]
    return jnp.cos(angles)[:, None, :], jnp.sin(angles)[:, None, :]


def rotate(values, cosine, sine):
    rows, columns = values.shape
    halves = values.reshape(rows, columns // HD, 2, HD // 2)
    front, back = halves[:, :, 0, :], halves[:, :, 1, :]
    turned = jnp.stack([front * cosine - back * sine, back * cosine + front * sine], axis=2)
    return turned.reshape(rows, columns)


def visible(begins, places):
    inside = (places[None, :] >= begins[:, None]) & (places[None, :] < begins[:, None] + PIECE)
    shared = jnp.any(inside[:, :, None] & inside[:, None, :], axis=0)
    return (places[None, :] <= places[:, None]) | shared


def attention_scores(query, key, bias):
    return mm_nt(query * jnp.asarray(1.0 / math.sqrt(HD), BF), key) + bias


def pair_specs(rows, count):
    return [pl.BlockSpec((rows, 2 * HD), lambda i: (0, i)) for _ in range(count)]


def attend_forward(query, key, value, bias):
    rows, columns = query.shape
    block = min(256, rows)

    def kernel(query_ref, key_ref, value_ref, bias_ref, out_ref, totals_ref):
        for head in range(2):
            lanes = slice(head * HD, (head + 1) * HD)
            k, v = key_ref[:, lanes], value_ref[:, lanes]
            for start in range(0, rows, block):
                now = slice(start, start + block)
                scores = attention_scores(query_ref[now, lanes], k, bias_ref[now, :])
                top = jnp.max(scores, axis=-1, keepdims=True)
                powers = jnp.exp(scores - top)
                total = jnp.sum(powers, axis=-1, keepdims=True)
                out_ref[now, lanes] = (mm(powers.astype(BF), v) * (1.0 / total)).astype(BF)
                totals_ref[now, lanes] = jnp.broadcast_to(top + jnp.log(total), (block, HD))

    return pl.pallas_call(
        kernel,
        grid=(columns // (2 * HD),),
        in_specs=pair_specs(rows, 3) + [pl.BlockSpec((rows, rows), lambda i: (0, 0))],
        out_specs=pair_specs(rows, 2),
        out_shape=[jax.ShapeDtypeStruct((rows, columns), BF), jax.ShapeDtypeStruct((rows, columns), F32)],
        compiler_params=pltpu.CompilerParams(vmem_limit_bytes=40 * 1024 * 1024),
        cost_estimate=pl.CostEstimate(
            flops=16 * rows * rows * columns,
            transcendentals=rows * rows * columns // HD,
            bytes_accessed=8 * rows * columns + 4 * rows * rows,
        ),
    )(query, key, value, bias)


def attend_backward(query, key, value, totals, grad, bias, cosine, sine):
    rows, columns = query.shape
    block = min(256, rows)
    scale = 1.0 / math.sqrt(HD)

    def kernel(query_ref, key_ref, value_ref, totals_ref, grad_ref, bias_ref, cos_ref, sin_ref, dq_ref, dk_ref, dv_ref, q_acc, k_acc):
        lane = lax.broadcasted_iota(jnp.int32, (rows, 2 * HD), 1)
        front = lane % HD < HD // 2

        def turned_back(values):
            other = jnp.where(front, pltpu.roll(values, 2 * HD - HD // 2, 1), pltpu.roll(values, HD // 2, 1))
            return (values * cos_ref[...] + other * sin_ref[...]).astype(BF)

        for head in range(2):
            lanes = slice(head * HD, (head + 1) * HD)
            k, v = key_ref[:, lanes], value_ref[:, lanes]
            k_sum = jnp.zeros((HD, rows), F32)
            v_sum = jnp.zeros((HD, rows), F32)
            for start in range(0, rows, block):
                now = slice(start, start + block)
                q, g = query_ref[now, lanes], grad_ref[now, lanes]
                total = totals_ref[now, head * HD : head * HD + 1]
                probs = jnp.exp(attention_scores(q, k, bias_ref[now, :]) - total)
                v_sum += mm_t(g, probs.astype(BF))
                grad_probs = mm_nt(g, v)
                centre = jnp.sum(probs * grad_probs, axis=-1, keepdims=True)
                grad_scores = (probs * (grad_probs - centre)).astype(BF)
                q_acc[now, lanes] = mm(grad_scores, k) * scale
                k_sum += mm_t(q, grad_scores)
            k_acc[:, lanes] = k_sum.T * scale
            dv_ref[:, lanes] = v_sum.T.astype(BF)
        dq_ref[...] = turned_back(q_acc[...])
        dk_ref[...] = turned_back(k_acc[...])

    return pl.pallas_call(
        kernel,
        grid=(columns // (2 * HD),),
        in_specs=pair_specs(rows, 5)
        + [pl.BlockSpec((rows, rows), lambda i: (0, 0))]
        + [pl.BlockSpec((rows, 2 * HD), lambda i: (0, 0))] * 2,
        out_specs=pair_specs(rows, 3),
        out_shape=[jax.ShapeDtypeStruct((rows, columns), BF)] * 3,
        scratch_shapes=[pltpu.VMEM((rows, 2 * HD), F32)] * 2,
        compiler_params=pltpu.CompilerParams(vmem_limit_bytes=48 * 1024 * 1024),
        cost_estimate=pl.CostEstimate(
            flops=30 * rows * rows * columns,
            transcendentals=rows * rows * columns // HD,
            bytes_accessed=14 * rows * columns + 4 * rows * rows,
        ),
    )(query, key, value, totals, grad, bias, cosine, sine)


def norm_forward(values):
    factor = lax.rsqrt(jnp.mean(values * values, axis=-1, keepdims=True) + EPS)
    return values * factor, factor


def norm_backward(unit, factor, gain, grad):
    scaled = grad * gain
    back = factor * (scaled - unit * jnp.mean(scaled * unit, axis=-1, keepdims=True))
    return back, jnp.sum(grad * unit, axis=0)


def place(pieces, targets, blocks, parts, axis):
    rows, columns = pieces[0][0].shape[1], pieces[0][0].shape[2] // parts
    total = len(pieces)

    def kernel(targets_ref, *refs):
        ins, outs = refs[:total], refs[total:]
        i = pl.program_id(0)
        for at, ref in enumerate(ins):

            @pl.when(i == at)
            def _():
                for j, out in enumerate(outs):
                    out[...] = ref[:, j * columns : (j + 1) * columns].astype(F32)

    def go(i, t):
        return (0, t[i]) if axis == 1 else (t[i], 0)

    shape = (rows, columns * blocks) if axis == 1 else (rows * blocks, columns)
    return pl.pallas_call(
        kernel,
        grid_spec=pltpu.PrefetchScalarGridSpec(
            num_scalar_prefetch=1,
            grid=(total,),
            in_specs=[
                pl.BlockSpec((None, rows, parts * columns), lambda i, t, at=at: (at, 0, 0)) for _, at in pieces
            ],
            out_specs=[pl.BlockSpec((rows, columns), go) for _ in range(parts)],
        ),
        out_shape=[jax.ShapeDtypeStruct(shape, F32) for _ in range(parts)],
        compiler_params=pltpu.CompilerParams(vmem_limit_bytes=32 * 1024 * 1024),
        cost_estimate=pl.CostEstimate(
            flops=0, transcendentals=0, bytes_accessed=6 * parts * rows * columns * blocks
        ),
    )(targets, *[array for array, _ in pieces])


def body(n_shard, n_ctx, n_tp, *arguments):
    (tokens, piece_starts, gain1, w_query, w_key, w_value, w_out, gain2, w_gate, w_up, w_down, cotangent) = arguments
    sequences, rows, width = tokens.shape
    assert sequences == 1
    z, c, t = lax.axis_index("shard"), lax.axis_index("ctx"), lax.axis_index("tp")
    short = rows // n_tp
    top = n_shard // 2
    high, low = z // top, z % top

    offsets = [(o, p) for o in order_of(n_ctx) for p in order_of(n_tp)]
    places = jnp.concatenate(
        [(c ^ o) * rows + (t ^ p) * short + jnp.arange(short, dtype=jnp.int32) for o, p in offsets]
    )
    bias = jnp.where(visible(piece_starts[0], places), 0.0, -1e30).astype(F32)
    cosine, sine = rope_tables(places)
    back_cosine = jnp.tile(cosine[:, 0, :], (1, 4))
    back_sine = jnp.tile(jnp.concatenate([sine[:, 0, :], -sine[:, 0, :]], axis=1), (1, 2))

    def own_first(values):
        return jnp.concatenate(
            [lax.dynamic_slice_in_dim(values, (t ^ p) * short, short, axis=0) for p in order_of(n_tp)]
        )

    def as_placed(found):
        result = jnp.zeros_like(found)
        for at, p in enumerate(order_of(n_tp)):
            block = found[at * short : (at + 1) * short]
            result = lax.dynamic_update_slice_in_dim(result, block, (t ^ p) * short, axis=0)
        return result[None]

    owners = jnp.stack([c ^ o for o in order_of(n_ctx)]).astype(jnp.int32)
    both_halves = jnp.concatenate([2 * owners + high, 2 * owners + 1 - high]).astype(jnp.int32)

    far_bits, tp_bits = bits_of(n_ctx)[:-1], bits_of(n_tp)
    chips = n_ctx // 2
    half = width // 2

    def halves(values, axis, bit, size, dim=0):
        keep, give = jnp.split(values, 2, axis=dim)
        return [keep, flip(give, axis, bit, size)]

    def added(keep, come):
        return (keep.astype(F32) + come.astype(F32)).astype(BF)

    def core_give(values):
        return halves(values, "ctx", 1, n_ctx)

    def ctx_give(values):
        for bit in reversed(far_bits[1:]):
            values = reduce_step(values, "ctx", bit, n_ctx)
        return halves(values, "ctx", far_bits[0], n_ctx)

    def tp_give(values, dim):
        for bit in reversed(tp_bits[1:]):
            values = reduce_step(values, "tp", bit, n_tp, dim)
        return halves(values, "tp", tp_bits[0], n_tp, dim)

    def first_give(left, right=None):
        if right is None:
            left, right = left[:, :half], left[:, half:]
        return ctx_give(left) + tp_give(right.reshape(chips, n_tp * short, right.shape[1]), 1)

    def last_give(keep, come, other_keep, other_come):
        right = added(other_keep, other_come).reshape(chips * short, keep.shape[1])
        return tp_give(added(keep, come), 0) + ctx_give(right)

    def reduced(keep, come, other_keep, other_come):
        return jnp.concatenate([added(keep, come), added(other_keep, other_come)], axis=1)

    def ctx_ask(values):
        for bit in far_bits[:-1]:
            values = jnp.concatenate([values, flip(values, "ctx", bit, n_ctx)], axis=0)
        return [values, flip(values, "ctx", far_bits[-1], n_ctx)]

    def tp_ask(values, dim):
        for bit in tp_bits[:-1]:
            values = jnp.concatenate([values, flip(values, "tp", bit, n_tp)], axis=dim)
        return [values, flip(values, "tp", tp_bits[-1], n_tp)]

    def first_ask(values):
        return tp_ask(values[:, :half], 0) + ctx_ask(values[:, half:])

    def last_ask(own, come, other_own, other_come):
        right = jnp.concatenate([other_own, other_come], axis=0).reshape(chips, short, half)
        return ctx_ask(jnp.concatenate([own, come], axis=0)) + tp_ask(right, 1)

    def joined(own, come, other_own, other_come):
        left = jnp.concatenate([own, come], axis=0)
        right = jnp.concatenate([other_own, other_come], axis=1).reshape(left.shape)
        return jnp.concatenate([left, right], axis=1)

    def core_ask(values):
        return [values, flip(values, "ctx", 1, n_ctx)]

    def stacked(*parts):
        return jnp.concatenate(parts, axis=0)

    def pair(values):
        return flip(values, "shard", top, n_shard)

    block = width // n_shard
    low_order = order_of(top)
    low_bits = bits_of(top)
    planes = [[side * top + o for o in range(top)] for side in range(2)]

    def low_sum(values, dim):
        where = jnp.asarray([low_order.index(o) for o in range(top)], jnp.int32)
        size = values.shape[dim] // top
        parts = [lax.dynamic_slice_in_dim(values, where[low ^ o] * size, size, axis=dim) for o in range(top)]
        return lax.psum_scatter(
            jnp.concatenate(parts, axis=dim), "shard", scatter_dimension=dim, tiled=True, axis_index_groups=planes
        )

    def folded(values):
        starts = [(side * top + (low ^ o)) * block for o in low_order for side in range(2)]
        return jnp.concatenate([lax.dynamic_slice_in_dim(values, s, block, axis=1) for s in starts], axis=1)

    def unfolded(values):
        where = jnp.asarray([low_order.index(o) for o in range(top)], jnp.int32)
        starts = [(2 * where[low ^ o] + side) * block for side in range(2) for o in range(top)]
        return jnp.concatenate([lax.dynamic_slice_in_dim(values, s, block, axis=1) for s in starts], axis=1)

    def low_ask(values):
        blocks = [values]
        for bit in low_bits:
            blocks = blocks + [flip(v, "shard", bit, n_shard) for v in blocks]
        return blocks

    def low_give(values, dim):
        for bit in reversed(low_bits[1:]):
            values = reduce_step(values, "shard", bit, n_shard, dim)
        return halves(values, "shard", low_bits[0], n_shard, dim)

    def packed(tied, *lengths):
        cuts, at = [], 0
        for length in lengths:
            cuts.append(list(tied[at : at + length]))
            at += length
        assert at == len(tied)
        return cuts

    def core_two(pieces):
        return pieces + [flip(v, "ctx", 1, n_ctx) for v in pieces]

    def ctx_two(values):
        pieces = [values]
        for bit in far_bits:
            pieces = pieces + [flip(v, "ctx", bit, n_ctx) for v in pieces]
        return pieces

    def swap(values, axis):
        size = values.shape[axis] // 2
        keep = lax.dynamic_slice_in_dim(values, high * size, size, axis=axis)
        give = lax.dynamic_slice_in_dim(values, (1 - high) * size, size, axis=axis)
        return keep, give

    heads = w_query.shape[1] // n_ctx
    units = w_gate.shape[1] // n_ctx // 2

    def attn_slice(weight, axis):
        return lax.dynamic_slice_in_dim(weight, c * heads, heads, axis=axis)

    def wide_slice(weight, side, axis):
        return lax.dynamic_slice_in_dim(weight, (2 * c + side) * units, units, axis=axis)

    attn_pack = [attn_slice(w, 1) for w in (w_query, w_key, w_value)] + [attn_slice(w_out, 0).T]
    attn_full = lax.all_gather(jnp.concatenate(attn_pack, axis=1), "shard", axis=0, tiled=True)
    gains = lax.all_gather(jnp.stack([gain1, gain2]), "shard", axis=1, tiled=True).astype(F32)
    gain1_full, gain2_full = gains[0], gains[1]
    x = own_first(tokens[0]).astype(F32)
    unit1, factor1 = norm_forward(x)
    n1 = gather((unit1 * gain1_full).astype(BF), "ctx", n_ctx)
    x, unit1, factor1 = x[:short], unit1[:short], factor1[:short]
    seed_all = own_first(cotangent[0])
    seed = seed_all[:short]
    seed_all = folded(seed_all)
    dy_pair = ctx_ask(seed_all)

    def ordered(own, come, axis):
        return jnp.where(
            high == 0,
            jnp.concatenate([own, come], axis=axis),
            jnp.concatenate([come, own], axis=axis),
        )

    give_gate, give_up = wide_slice(w_gate, 1 - high, 1), wide_slice(w_up, 1 - high, 1)
    give_down = wide_slice(w_down, 1 - high, 0)
    own_gate, own_up, own_down = wide_slice(w_gate, high, 1), wide_slice(w_up, high, 1), wide_slice(w_down, high, 0)
    dy_far = pair(seed_all[:short])
    attn_full, n1, dy_far, give_gate, give_up, give_down, *dy_near = tie(
        attn_full, n1, dy_far, give_gate, give_up, give_down, *dy_pair
    )

    qkv_full, out_full = attn_full[:, : 3 * heads], attn_full[:, 3 * heads :]
    come_gate = pair(give_gate)
    dy_far = last_ask(*first_ask(dy_far))
    qkv = mm(n1, qkv_full)
    query = rotate(qkv[:, :heads], cosine, sine).astype(BF)
    key = rotate(qkv[:, heads : 2 * heads], cosine, sine).astype(BF)
    value = qkv[:, 2 * heads :].astype(BF)
    mixed, totals = attend_forward(query, key, value, bias)
    mixed, come_gate, give_up, give_down, *rest = tie(mixed, come_gate, give_up, give_down, *dy_far, *dy_near)
    dy_far, dy_near = rest[:4], rest[4:]
    come_up = pair(give_up)
    gate_blocks = low_ask(ordered(own_gate, come_gate, 0))
    partial = core_give(mm_nt(mixed, out_full).astype(BF))
    partial = first_give(added(*partial))
    partial = last_give(*tie(*partial))
    come_up, give_down, n1, *rest = tie(come_up, give_down, n1, *partial, *gate_blocks)
    partial, gate_blocks = rest[:4], rest[4:]
    up_blocks = low_ask(ordered(own_up, come_up, 0))
    h1 = x + reduced(*partial).astype(F32)
    unit2, factor2 = norm_forward(h1)
    n2_short = folded((unit2 * gain2_full).astype(BF))
    n2_far = pair(n2_short)
    near = first_ask(n2_short)
    *near, gate_full = tie(*near, stacked(*gate_blocks))
    near = last_ask(*near)
    n1_folded = folded(n1)
    dy_near = stacked(*dy_near)
    n2_far, give_down, n1_folded, gate_full, dy_near, *rest = tie(
        n2_far, give_down, n1_folded, gate_full, dy_near, *near, *up_blocks, *dy_far
    )
    near, up_blocks, dy_far = rest[:4], rest[4:-4], rest[-4:]

    come_down = pair(give_down)
    far = first_ask(n2_far)
    near = core_ask(joined(*near))
    up_full = stacked(*up_blocks)
    up_full, *rest = tie(up_full, *near, *far)
    near, far = rest[:2], rest[2:]
    wide_full = jnp.concatenate([gate_full, up_full], axis=1)
    n2_near = stacked(*near)

    def wide_forward(n2):
        both = mm(n2, wide_full)
        gate, up = both[:, :units], both[:, units:]
        sigma = jax.nn.sigmoid(gate)
        silu = gate * sigma
        return (silu * up).astype(BF), silu, up * (sigma * (1.0 + gate * (1.0 - sigma)))

    def wide_backward(dy, silu, slope):
        grad_hidden = mm_nt(dy, down_full)
        return (grad_hidden * slope).astype(BF), (grad_hidden * silu).astype(BF)

    def wide_input(grad_gate, grad_up):
        return mm_nt(jnp.concatenate([grad_gate, grad_up], axis=1), wide_full).astype(BF)

    far = last_ask(*far)
    forward_near = wide_forward(n2_near)
    come_down, n2_near, *rest = tie(come_down, n2_near, *forward_near, *far, *dy_far)
    forward_near, far, dy_far = rest[:3], rest[3:7], rest[7:]
    down_blocks = low_ask(ordered(own_down, come_down, 1))
    far = core_ask(joined(*far))
    dy_near = core_ask(dy_near)
    dy_far = core_ask(joined(*dy_far))
    *far, dy_one, dy_two, one, two = tie(*far, *dy_near, *dy_far)
    dy_near = stacked(dy_one, dy_two)
    dy_far = [one, two]
    n2_far = stacked(*far)
    forward_far = wide_forward(n2_far)
    down_part = mm_t(forward_near[0], dy_near)
    n2_far, dy_near, down_part, *rest = tie(n2_far, dy_near, down_part, *forward_far, *dy_far, *down_blocks)
    forward_far, dy_far, down_full = rest[:3], rest[3:5], jnp.concatenate(rest[5:], axis=1)
    gate_near, up_near = wide_backward(dy_near, *forward_near[1:])
    near = wide_input(gate_near, up_near)
    near, gate_near, n2_near, *dy_far = tie(near, gate_near, n2_near, *dy_far)
    near = core_give(near)
    dy_far = stacked(*dy_far)
    gate_far, up_far = wide_backward(dy_far, *forward_far[1:])
    gate_far, up_far, dy_far, n2_near, *near = tie(gate_far, up_far, dy_far, n2_near, *near)
    near = first_give(added(*near))
    hidden_near, hidden_far = forward_near[0], forward_far[0]
    grad_down = (down_part + mm_t(hidden_far, dy_far)).astype(BF)
    down_low = low_sum(grad_down, 1)
    far = wide_input(gate_far, up_far)
    far, grad_down, n2_far, n2_near, *near = tie(far, grad_down, n2_far, n2_near, *near)
    far = core_give(far)
    near = last_give(*near)
    gate_near, hidden_near, n2_near, down_low, *rest = tie(gate_near, hidden_near, n2_near, down_low, *far, *near)
    far, near = packed(rest, 2, 4)
    near = reduced(*near)
    far = first_give(added(*far))
    down_keep, down_give = swap(down_low, 1)
    down_come = pair(down_give)
    near, gate_near, hidden_near, n2_far, n2_near, *far = tie(near, gate_near, hidden_near, n2_far, n2_near, *far)
    far = last_give(*far)
    n2_near, n2_far, up_near, gate_near, hidden_near, down_keep, down_come, *far = tie(
        n2_near, n2_far, up_near, gate_near, hidden_near, down_keep, down_come, *far
    )

    far = pair(reduced(*far))
    down_keep = ctx_two(down_keep)
    grad_gate_w = (mm_t(n2_near, gate_near) + mm_t(n2_far, gate_far)).astype(BF)
    middle = n1.shape[0] // 2
    result_keep, result_give = [
        mm(stacked(hidden_near[part], hidden_far[part]), down_full).astype(BF)
        for part in (slice(None, middle), slice(middle, None))
    ]
    far, grad_gate_w, up_near, n2_near, n2_far, result_keep, result_give, *down_keep = tie(
        far, grad_gate_w, up_near, n2_near, n2_far, result_keep, result_give, *down_keep
    )
    gate_low = low_give(grad_gate_w, 0)
    grad_n2 = unfolded(near.astype(F32) + far.astype(F32))
    back2, grad_norm2 = norm_backward(unit2, factor2, gain2_full, grad_n2)
    grad_h1 = seed.astype(F32) + back2
    dh1 = last_ask(*first_ask(grad_h1.astype(BF)))
    grad_up_w = (mm_t(n2_near, up_near) + mm_t(n2_far, up_far)).astype(BF)
    result = added(result_keep, flip(result_give, "ctx", 1, n_ctx))
    grad_up_w, result, *rest = tie(grad_up_w, result, *dh1, *gate_low)
    dh1, gate_low = packed(rest, 4, 2)

    dh1_own = joined(*dh1)
    dh1_come = flip(dh1_own, "ctx", 1, n_ctx)
    up_low = low_give(grad_up_w, 0)
    down_keep = core_two(down_keep)
    mixed_own, out_own = mm(dh1_own, out_full).astype(BF), mm_t(mixed[:middle], dh1_own)
    result, dh1_come, mixed_own, out_own, *rest = tie(result, dh1_come, mixed_own, out_own, *gate_low, *down_keep)
    gate_low, down_keep = packed(rest, 2, 2 * chips)
    result = first_give(result[:middle], result[middle:])
    grad_out = (out_own + mm_t(mixed[middle:], dh1_come)).astype(BF)
    share_out = lax.psum_scatter(grad_out, "shard", scatter_dimension=1, tiled=True)
    dh1_come, grad_out = tie(dh1_come, grad_out)
    gate_keep, gate_give = swap(added(*gate_low), 0)
    grad_mixed = stacked(mixed_own, mm(dh1_come, out_full).astype(BF))
    gate_come = pair(gate_give)
    gate_keep = ctx_two(gate_keep)
    dq, dk, dv = attend_backward(query, key, value, totals, grad_mixed, bias, back_cosine, back_sine)
    dq, dk, dv, gate_come, down_come, *rest = tie(dq, dk, dv, gate_come, down_come, *result, *gate_keep, *up_low)
    result, gate_keep, up_low = packed(rest, 4, chips, 2)
    dqkv = jnp.concatenate([dq, dk, dv], axis=1)
    grad_qkv = mm_t(n1_folded, dqkv).astype(BF)

    dqkv, grad_qkv, gate_come, down_come, share_out, *rest = tie(
        dqkv, grad_qkv, gate_come, down_come, share_out, *result, *up_low, *gate_keep
    )
    result, up_low, gate_keep = packed(rest, 4, 2, chips)
    share_qkv = low_give(grad_qkv, 0)
    grad_n1 = core_give(mm_nt(dqkv, qkv_full).astype(BF))
    up_keep, up_give = swap(added(*up_low), 0)
    up_come = pair(up_give)
    result = last_give(*result)
    three = jnp.stack([gate_come, down_come, up_keep])
    three, *rest = tie(three, *grad_n1, *result, *gate_keep)
    grad_n1, result, gate_keep = packed(rest, 2, 4, chips)
    three, gate_keep = ctx_two(three), core_two(gate_keep)
    grad_n1 = added(*grad_n1)
    result_near, result_far = added(*result[:2]), pair(added(*result[2:]))
    up_come, grad_n1, result_near, result_far, *rest = tie(
        up_come, grad_n1, result_near, result_far, *share_qkv, *three, *gate_keep, *ctx_two(share_out)
    )
    share_qkv, three, gate_keep, share_out = packed(rest, 2, chips, 2 * chips, chips)
    share_qkv, qkv_give = swap(added(*share_qkv), 0)
    qkv_come = pair(qkv_give)
    grad_n1 = first_give(grad_n1)
    three = core_two(three)
    output = (h1 + unfolded(result_near.astype(F32) + result_far.astype(F32))).astype(BF)
    up_come, output, *rest = tie(up_come, output, *grad_n1, *three)
    grad_n1, three = packed(rest, 4, 2 * chips)
    grad_n1 = last_give(*grad_n1)
    up_come, output = ctx_two(up_come), tp_ask(output, 0)
    (grad_g,) = place(
        [(v[None], 0) for v in gate_keep] + [(v, 0) for v in three], both_halves, 2 * n_ctx, 1, 1
    )
    (grad_d,) = place(
        [(v[None], 0) for v in down_keep] + [(v, 1) for v in three], both_halves, 2 * n_ctx, 1, 0
    )
    qkv_come, share_qkv, grad_g, grad_d, *rest = tie(
        qkv_come, share_qkv, grad_g, grad_d, *grad_n1, *up_come, *output
    )
    grad_n1, up_come, output = packed(rest, 4, chips, 2)
    share_qkv = ctx_two(added(share_qkv, qkv_come))
    back1, grad_norm1 = norm_backward(unit1, factor1, gain1_full, reduced(*grad_n1).astype(F32))
    input_grad, output = tp_ask((grad_h1 + back1).astype(BF), 0), as_placed(stacked(*output))
    norms = jnp.stack([grad_norm1, grad_norm2]).reshape(-1, 128)

    def met(values, axis, bits, size):
        for bit in bits:
            values = values + flip(values, axis, bit, size)
        return values

    norms, up_come = met(norms, "tp", tp_bits, n_tp), core_two(up_come)
    norms, output, *rest = tie(norms, output, *share_qkv, *input_grad, *up_come)
    share_qkv, input_grad, up_come = packed(rest, chips, 2, 2 * chips)
    norms, share_qkv, share_out = met(norms, "ctx", [1], n_ctx), core_two(share_qkv), core_two(share_out)
    norms, *rest = tie(norms, *share_qkv, *share_out)
    share_qkv, share_out = packed(rest, 2 * chips, 2 * chips)
    norms = met(norms, "ctx", far_bits, n_ctx)
    input_grad = as_placed(stacked(*input_grad))
    grad_q, grad_k, grad_v = place([(v[None], 0) for v in share_qkv], owners, n_ctx, 3, 1)
    grad_q, grad_k, grad_v, norms = tie(grad_q, grad_k, grad_v, norms)
    norms = met(norms, "shard", low_bits, n_shard)
    (grad_u,) = place([(v, 2) for v in three] + [(v[None], 0) for v in up_come], both_halves, 2 * n_ctx, 1, 1)
    grad_u, norms = tie(grad_u, norms)
    norms = met(norms, "shard", [top], n_shard)
    (grad_o,) = place([(v[None], 0) for v in share_out], owners, n_ctx, 1, 0)
    norms = lax.dynamic_slice_in_dim(norms.reshape(2, width), z * block, block, axis=1)
    return (output, input_grad, norms[0], grad_q, grad_k, grad_v, grad_o, norms[1], grad_g, grad_u, grad_d)


def solution(mesh):
    n_shard, n_ctx, n_tp = mesh.shape["shard"], mesh.shape["ctx"], mesh.shape["tp"]

    def local(*arguments):
        return body(n_shard, n_ctx, n_tp, *arguments)

    return jax.shard_map(
        local,
        mesh=mesh,
        in_specs=(
            P("shard", "ctx", None),
            P("shard", None),
            P("shard"),
            P("shard", "tp"),
            P("shard", "tp"),
            P("shard", "tp"),
            P("tp", "shard"),
            P("shard"),
            P("shard", "tp"),
            P("shard", "tp"),
            P("tp", "shard"),
            P("shard", "ctx", None),
        ),
        out_specs=(
            P("shard", "ctx", None),
            P("shard", "ctx", None),
            P("shard"),
            P("shard", "tp"),
            P("shard", "tp"),
            P("shard", "tp"),
            P("tp", "shard"),
            P("shard"),
            P("shard", "tp"),
            P("shard", "tp"),
            P("tp", "shard"),
        ),
        check_vma=False,
    )
```

```python
import math

import jax
import jax.numpy as jnp
from jax import lax
from jax.experimental import pallas as pl
from jax.experimental.pallas import tpu as pltpu
from jax.sharding import PartitionSpec as P

HD = 64
PIECE = 256

EPS = 1e-05
ROPE_BASE = 130000.0
BF = jnp.bfloat16
F32 = jnp.float32


def flip(values, axis, bit, size):
    return lax.ppermute(values, axis, [(i, i ^ bit) for i in range(size)])


def bits_of(size):
    found, bit = [], size // 2
    while bit >= 1:
        found.append(bit)
        bit //= 2
    return found


def order_of(size):
    order = [0]
    for bit in bits_of(size):
        order = order + [o | bit for o in order]
    return order


def tie(*values):
    return lax.optimization_barrier(values)


def gather(block, axis, size, dim=0):
    for bit in bits_of(size):
        block = jnp.concatenate([block, flip(block, axis, bit, size)], axis=dim)
    return block


def reduce_step(partial, axis, bit, size, dim=0):
    keep, give = jnp.split(partial, 2, axis=dim)
    come = flip(give, axis, bit, size)
    return (keep.astype(F32) + come.astype(F32)).astype(BF)


def mm(left, right):
    return jnp.dot(left, right, preferred_element_type=F32)


def mm_t(left, right):
    return lax.dot_general(left, right, (((0,), (0,)), ((), ())), preferred_element_type=F32)


def mm_nt(left, right):
    return lax.dot_general(left, right, (((1,), (1,)), ((), ())), preferred_element_type=F32)


def rope_tables(positions):
    frequency = jnp.power(ROPE_BASE, -2.0 * jnp.arange(HD // 2, dtype=F32) / HD)
    angles = positions.astype(F32)[:, None] * frequency[None, :]
    return jnp.cos(angles)[:, None, :], jnp.sin(angles)[:, None, :]


def rotate(values, cosine, sine):
    rows, columns = values.shape
    halves = values.reshape(rows, columns // HD, 2, HD // 2)
    front, back = halves[:, :, 0, :], halves[:, :, 1, :]
    turned = jnp.stack([front * cosine - back * sine, back * cosine + front * sine], axis=2)
    return turned.reshape(rows, columns)


def visible(begins, places):
    inside = (places[None, :] >= begins[:, None]) & (places[None, :] < begins[:, None] + PIECE)
    shared = jnp.any(inside[:, :, None] & inside[:, None, :], axis=0)
    return (places[None, :] <= places[:, None]) | shared


def attention_scores(query, key, bias):
    return mm_nt(query * jnp.asarray(1.0 / math.sqrt(HD), BF), key) + bias


def pair_specs(rows, count):
    return [pl.BlockSpec((rows, 2 * HD), lambda i: (0, i)) for _ in range(count)]


def attend_forward(query, key, value, bias):
    rows, columns = query.shape
    block = min(512, rows)

    def kernel(query_ref, key_ref, value_ref, bias_ref, out_ref, totals_ref):
        for head in range(2):
            lanes = slice(head * HD, (head + 1) * HD)
            k, v = key_ref[:, lanes], value_ref[:, lanes]
            for start in range(0, rows, block):
                now = slice(start, start + block)
                scores = attention_scores(query_ref[now, lanes], k, bias_ref[now, :])
                top = jnp.max(scores, axis=-1, keepdims=True)
                powers = jnp.exp(scores - top)
                total = jnp.sum(powers, axis=-1, keepdims=True)
                out_ref[now, lanes] = (mm(powers.astype(BF), v) * (1.0 / total)).astype(BF)
                totals_ref[now, lanes] = jnp.broadcast_to(top + jnp.log(total), (block, HD))

    return pl.pallas_call(
        kernel,
        grid=(columns // (2 * HD),),
        in_specs=pair_specs(rows, 3) + [pl.BlockSpec((rows, rows), lambda i: (0, 0))],
        out_specs=pair_specs(rows, 2),
        out_shape=[jax.ShapeDtypeStruct((rows, columns), BF), jax.ShapeDtypeStruct((rows, columns), F32)],
        compiler_params=pltpu.CompilerParams(vmem_limit_bytes=40 * 1024 * 1024),
        cost_estimate=pl.CostEstimate(
            flops=16 * rows * rows * columns,
            transcendentals=rows * rows * columns // HD,
            bytes_accessed=8 * rows * columns + 4 * rows * rows,
        ),
    )(query, key, value, bias)


def attend_backward(query, key, value, totals, grad, bias, cosine, sine):
    rows, columns = query.shape
    block = min(512, rows)
    scale = 1.0 / math.sqrt(HD)

    def kernel(query_ref, key_ref, value_ref, totals_ref, grad_ref, bias_ref, cos_ref, sin_ref, dq_ref, dk_ref, dv_ref, q_acc, k_acc):
        lane = lax.broadcasted_iota(jnp.int32, (rows, 2 * HD), 1)
        front = lane % HD < HD // 2

        def turned_back(values):
            other = jnp.where(front, pltpu.roll(values, 2 * HD - HD // 2, 1), pltpu.roll(values, HD // 2, 1))
            return (values * cos_ref[...] + other * sin_ref[...]).astype(BF)

        for head in range(2):
            lanes = slice(head * HD, (head + 1) * HD)
            k, v = key_ref[:, lanes], value_ref[:, lanes]
            k_sum = jnp.zeros((HD, rows), F32)
            v_sum = jnp.zeros((HD, rows), F32)
            for start in range(0, rows, block):
                now = slice(start, start + block)
                q, g = query_ref[now, lanes], grad_ref[now, lanes]
                total = totals_ref[now, head * HD : head * HD + 1]
                probs = jnp.exp(attention_scores(q, k, bias_ref[now, :]) - total)
                v_sum += mm_t(g, probs.astype(BF))
                grad_probs = mm_nt(g, v)
                centre = jnp.sum(probs * grad_probs, axis=-1, keepdims=True)
                grad_scores = (probs * (grad_probs - centre)).astype(BF)
                q_acc[now, lanes] = mm(grad_scores, k) * scale
                k_sum += mm_t(q, grad_scores)
            k_acc[:, lanes] = k_sum.T * scale
            dv_ref[:, lanes] = v_sum.T.astype(BF)
        dq_ref[...] = turned_back(q_acc[...])
        dk_ref[...] = turned_back(k_acc[...])

    return pl.pallas_call(
        kernel,
        grid=(columns // (2 * HD),),
        in_specs=pair_specs(rows, 5)
        + [pl.BlockSpec((rows, rows), lambda i: (0, 0))]
        + [pl.BlockSpec((rows, 2 * HD), lambda i: (0, 0))] * 2,
        out_specs=pair_specs(rows, 3),
        out_shape=[jax.ShapeDtypeStruct((rows, columns), BF)] * 3,
        scratch_shapes=[pltpu.VMEM((rows, 2 * HD), F32)] * 2,
        compiler_params=pltpu.CompilerParams(vmem_limit_bytes=48 * 1024 * 1024),
        cost_estimate=pl.CostEstimate(
            flops=30 * rows * rows * columns,
            transcendentals=rows * rows * columns // HD,
            bytes_accessed=14 * rows * columns + 4 * rows * rows,
        ),
    )(query, key, value, totals, grad, bias, cosine, sine)


def norm_forward(values):
    factor = lax.rsqrt(jnp.mean(values * values, axis=-1, keepdims=True) + EPS)
    return values * factor, factor


def norm_backward(unit, factor, gain, grad):
    scaled = grad * gain
    back = factor * (scaled - unit * jnp.mean(scaled * unit, axis=-1, keepdims=True))
    return back, jnp.sum(grad * unit, axis=0)


def place(pieces, targets, blocks, parts, axis):
    rows, columns = pieces[0][0].shape[1], pieces[0][0].shape[2] // parts
    total = len(pieces)

    def kernel(targets_ref, *refs):
        ins, outs = refs[:total], refs[total:]
        i = pl.program_id(0)
        for at, ref in enumerate(ins):

            @pl.when(i == at)
            def _():
                for j, out in enumerate(outs):
                    out[...] = ref[:, j * columns : (j + 1) * columns].astype(F32)

    def go(i, t):
        return (0, t[i]) if axis == 1 else (t[i], 0)

    shape = (rows, columns * blocks) if axis == 1 else (rows * blocks, columns)
    return pl.pallas_call(
        kernel,
        grid_spec=pltpu.PrefetchScalarGridSpec(
            num_scalar_prefetch=1,
            grid=(total,),
            in_specs=[
                pl.BlockSpec((None, rows, parts * columns), lambda i, t, at=at: (at, 0, 0)) for _, at in pieces
            ],
            out_specs=[pl.BlockSpec((rows, columns), go) for _ in range(parts)],
        ),
        out_shape=[jax.ShapeDtypeStruct(shape, F32) for _ in range(parts)],
        compiler_params=pltpu.CompilerParams(vmem_limit_bytes=32 * 1024 * 1024),
        cost_estimate=pl.CostEstimate(
            flops=0, transcendentals=0, bytes_accessed=6 * parts * rows * columns * blocks
        ),
    )(targets, *[array for array, _ in pieces])


def body(n_shard, n_ctx, n_tp, *arguments):
    (tokens, piece_starts, gain1, w_query, w_key, w_value, w_out, gain2, w_gate, w_up, w_down, cotangent) = arguments
    sequences, rows, width = tokens.shape
    assert sequences == 1
    z, c, t = lax.axis_index("shard"), lax.axis_index("ctx"), lax.axis_index("tp")
    short = rows // n_tp
    top = n_shard // 2
    high, low = z // top, z % top

    offsets = [(o, p) for o in order_of(n_ctx) for p in order_of(n_tp)]
    places = jnp.concatenate(
        [(c ^ o) * rows + (t ^ p) * short + jnp.arange(short, dtype=jnp.int32) for o, p in offsets]
    )
    bias = jnp.where(visible(piece_starts[0], places), 0.0, -1e30).astype(F32)
    cosine, sine = rope_tables(places)
    back_cosine = jnp.tile(cosine[:, 0, :], (1, 4))
    back_sine = jnp.tile(jnp.concatenate([sine[:, 0, :], -sine[:, 0, :]], axis=1), (1, 2))

    def own_first(values):
        return jnp.concatenate(
            [lax.dynamic_slice_in_dim(values, (t ^ p) * short, short, axis=0) for p in order_of(n_tp)]
        )

    def as_placed(found):
        result = jnp.zeros_like(found)
        for at, p in enumerate(order_of(n_tp)):
            block = found[at * short : (at + 1) * short]
            result = lax.dynamic_update_slice_in_dim(result, block, (t ^ p) * short, axis=0)
        return result[None]

    owners = jnp.stack([c ^ o for o in order_of(n_ctx)]).astype(jnp.int32)
    both_halves = jnp.concatenate([2 * owners + high, 2 * owners + 1 - high]).astype(jnp.int32)

    far_bits, tp_bits = bits_of(n_ctx)[:-1], bits_of(n_tp)
    chips = n_ctx // 2
    half = width // 2

    def halves(values, axis, bit, size, dim=0):
        keep, give = jnp.split(values, 2, axis=dim)
        return [keep, flip(give, axis, bit, size)]

    def added(keep, come):
        return (keep.astype(F32) + come.astype(F32)).astype(BF)

    def core_give(values):
        return halves(values, "ctx", 1, n_ctx)

    def ctx_give(values):
        for bit in reversed(far_bits[1:]):
            values = reduce_step(values, "ctx", bit, n_ctx)
        return halves(values, "ctx", far_bits[0], n_ctx)

    def tp_give(values, dim):
        for bit in reversed(tp_bits[1:]):
            values = reduce_step(values, "tp", bit, n_tp, dim)
        return halves(values, "tp", tp_bits[0], n_tp, dim)

    def first_give(left, right=None):
        if right is None:
            left, right = left[:, :half], left[:, half:]
        return ctx_give(left) + tp_give(right.reshape(chips, n_tp * short, right.shape[1]), 1)

    def last_give(keep, come, other_keep, other_come):
        right = added(other_keep, other_come).reshape(chips * short, keep.shape[1])
        return tp_give(added(keep, come), 0) + ctx_give(right)

    def reduced(keep, come, other_keep, other_come):
        return jnp.concatenate([added(keep, come), added(other_keep, other_come)], axis=1)

    def ctx_ask(values):
        for bit in far_bits[:-1]:
            values = jnp.concatenate([values, flip(values, "ctx", bit, n_ctx)], axis=0)
        return [values, flip(values, "ctx", far_bits[-1], n_ctx)]

    def tp_ask(values, dim):
        for bit in tp_bits[:-1]:
            values = jnp.concatenate([values, flip(values, "tp", bit, n_tp)], axis=dim)
        return [values, flip(values, "tp", tp_bits[-1], n_tp)]

    def first_ask(values):
        return tp_ask(values[:, :half], 0) + ctx_ask(values[:, half:])

    def last_ask(own, come, other_own, other_come):
        right = jnp.concatenate([other_own, other_come], axis=0).reshape(chips, short, half)
        return ctx_ask(jnp.concatenate([own, come], axis=0)) + tp_ask(right, 1)

    def joined(own, come, other_own, other_come):
        left = jnp.concatenate([own, come], axis=0)
        right = jnp.concatenate([other_own, other_come], axis=1).reshape(left.shape)
        return jnp.concatenate([left, right], axis=1)

    def core_ask(values):
        return [values, flip(values, "ctx", 1, n_ctx)]

    def stacked(*parts):
        return jnp.concatenate(parts, axis=0)

    def pair(values):
        return flip(values, "shard", top, n_shard)

    block = width // n_shard
    low_order = order_of(top)
    low_bits = bits_of(top)
    planes = [[side * top + o for o in range(top)] for side in range(2)]

    def low_sum(values, dim):
        where = jnp.asarray([low_order.index(o) for o in range(top)], jnp.int32)
        size = values.shape[dim] // top
        parts = [lax.dynamic_slice_in_dim(values, where[low ^ o] * size, size, axis=dim) for o in range(top)]
        return lax.psum_scatter(
            jnp.concatenate(parts, axis=dim), "shard", scatter_dimension=dim, tiled=True, axis_index_groups=planes
        )

    def folded(values):
        starts = [(side * top + (low ^ o)) * block for o in low_order for side in range(2)]
        return jnp.concatenate([lax.dynamic_slice_in_dim(values, s, block, axis=1) for s in starts], axis=1)

    def unfolded(values):
        where = jnp.asarray([low_order.index(o) for o in range(top)], jnp.int32)
        starts = [(2 * where[low ^ o] + side) * block for side in range(2) for o in range(top)]
        return jnp.concatenate([lax.dynamic_slice_in_dim(values, s, block, axis=1) for s in starts], axis=1)

    def low_ask(values):
        blocks = [values]
        for bit in low_bits:
            blocks = blocks + [flip(v, "shard", bit, n_shard) for v in blocks]
        return blocks

    def low_give(values, dim):
        for bit in reversed(low_bits[1:]):
            values = reduce_step(values, "shard", bit, n_shard, dim)
        return halves(values, "shard", low_bits[0], n_shard, dim)

    def packed(tied, *lengths):
        cuts, at = [], 0
        for length in lengths:
            cuts.append(list(tied[at : at + length]))
            at += length
        assert at == len(tied)
        return cuts

    def core_two(pieces):
        return pieces + [flip(v, "ctx", 1, n_ctx) for v in pieces]

    def ctx_two(values):
        pieces = [values]
        for bit in far_bits:
            pieces = pieces + [flip(v, "ctx", bit, n_ctx) for v in pieces]
        return pieces

    def swap(values, axis):
        size = values.shape[axis] // 2
        keep = lax.dynamic_slice_in_dim(values, high * size, size, axis=axis)
        give = lax.dynamic_slice_in_dim(values, (1 - high) * size, size, axis=axis)
        return keep, give

    heads = w_query.shape[1] // n_ctx
    units = w_gate.shape[1] // n_ctx // 2

    def attn_slice(weight, axis):
        return lax.dynamic_slice_in_dim(weight, c * heads, heads, axis=axis)

    def wide_slice(weight, side, axis):
        return lax.dynamic_slice_in_dim(weight, (2 * c + side) * units, units, axis=axis)

    attn_pack = [attn_slice(w, 1) for w in (w_query, w_key, w_value)] + [attn_slice(w_out, 0).T]
    attn_full = lax.all_gather(jnp.concatenate(attn_pack, axis=1), "shard", axis=0, tiled=True)
    gains = lax.all_gather(jnp.stack([gain1, gain2]), "shard", axis=1, tiled=True).astype(F32)
    gain1_full, gain2_full = gains[0], gains[1]
    x = own_first(tokens[0]).astype(F32)
    unit1, factor1 = norm_forward(x)
    n1 = gather((unit1 * gain1_full).astype(BF), "ctx", n_ctx)
    x, unit1, factor1 = x[:short], unit1[:short], factor1[:short]
    seed_all = own_first(cotangent[0])
    seed = seed_all[:short]
    seed_all = folded(seed_all)
    dy_pair = ctx_ask(seed_all)

    def ordered(own, come, axis):
        return jnp.where(
            high == 0,
            jnp.concatenate([own, come], axis=axis),
            jnp.concatenate([come, own], axis=axis),
        )

    give_gate, give_up = wide_slice(w_gate, 1 - high, 1), wide_slice(w_up, 1 - high, 1)
    give_down = wide_slice(w_down, 1 - high, 0)
    own_gate, own_up, own_down = wide_slice(w_gate, high, 1), wide_slice(w_up, high, 1), wide_slice(w_down, high, 0)
    dy_far = pair(seed_all[:short])
    attn_full, n1, dy_far, give_gate, give_up, give_down, *dy_near = tie(
        attn_full, n1, dy_far, give_gate, give_up, give_down, *dy_pair
    )

    qkv_full, out_full = attn_full[:, : 3 * heads], attn_full[:, 3 * heads :]
    come_gate = pair(give_gate)
    dy_far = last_ask(*first_ask(dy_far))
    qkv = mm(n1, qkv_full)
    query = rotate(qkv[:, :heads], cosine, sine).astype(BF)
    key = rotate(qkv[:, heads : 2 * heads], cosine, sine).astype(BF)
    value = qkv[:, 2 * heads :].astype(BF)
    mixed, totals = attend_forward(query, key, value, bias)
    mixed, come_gate, give_up, give_down, *rest = tie(mixed, come_gate, give_up, give_down, *dy_far, *dy_near)
    dy_far, dy_near = rest[:4], rest[4:]
    come_up = pair(give_up)
    gate_blocks = low_ask(ordered(own_gate, come_gate, 0))
    partial = core_give(mm_nt(mixed, out_full).astype(BF))
    partial = first_give(added(*partial))
    partial = last_give(*tie(*partial))
    come_up, give_down, n1, *rest = tie(come_up, give_down, n1, *partial, *gate_blocks)
    partial, gate_blocks = rest[:4], rest[4:]
    up_blocks = low_ask(ordered(own_up, come_up, 0))
    h1 = x + reduced(*partial).astype(F32)
    unit2, factor2 = norm_forward(h1)
    n2_short = folded((unit2 * gain2_full).astype(BF))
    n2_far = pair(n2_short)
    near = first_ask(n2_short)
    *near, gate_full = tie(*near, stacked(*gate_blocks))
    near = last_ask(*near)
    n1_folded = folded(n1)
    dy_near = stacked(*dy_near)
    n2_far, give_down, n1_folded, gate_full, dy_near, *rest = tie(
        n2_far, give_down, n1_folded, gate_full, dy_near, *near, *up_blocks, *dy_far
    )
    near, up_blocks, dy_far = rest[:4], rest[4:-4], rest[-4:]

    come_down = pair(give_down)
    far = first_ask(n2_far)
    near = core_ask(joined(*near))
    up_full = stacked(*up_blocks)
    up_full, *rest = tie(up_full, *near, *far)
    near, far = rest[:2], rest[2:]
    wide_full = jnp.concatenate([gate_full, up_full], axis=1)
    n2_near = stacked(*near)

    def wide_forward(n2):
        both = mm(n2, wide_full)
        gate, up = both[:, :units], both[:, units:]
        sigma = jax.nn.sigmoid(gate)
        silu = gate * sigma
        return (silu * up).astype(BF), silu, up * (sigma * (1.0 + gate * (1.0 - sigma)))

    def wide_backward(dy, silu, slope):
        grad_hidden = mm_nt(dy, down_full)
        return (grad_hidden * slope).astype(BF), (grad_hidden * silu).astype(BF)

    def wide_input(grad_gate, grad_up):
        return mm_nt(jnp.concatenate([grad_gate, grad_up], axis=1), wide_full).astype(BF)

    far = last_ask(*far)
    forward_near = wide_forward(n2_near)
    come_down, n2_near, *rest = tie(come_down, n2_near, *forward_near, *far, *dy_far)
    forward_near, far, dy_far = rest[:3], rest[3:7], rest[7:]
    down_blocks = low_ask(ordered(own_down, come_down, 1))
    far = core_ask(joined(*far))
    dy_near = core_ask(dy_near)
    dy_far = core_ask(joined(*dy_far))
    *far, dy_one, dy_two, one, two = tie(*far, *dy_near, *dy_far)
    dy_near = stacked(dy_one, dy_two)
    dy_far = [one, two]
    n2_far = stacked(*far)
    forward_far = wide_forward(n2_far)
    down_part = mm_t(forward_near[0], dy_near)
    n2_far, dy_near, down_part, *rest = tie(n2_far, dy_near, down_part, *forward_far, *dy_far, *down_blocks)
    forward_far, dy_far, down_full = rest[:3], rest[3:5], jnp.concatenate(rest[5:], axis=1)
    gate_near, up_near = wide_backward(dy_near, *forward_near[1:])
    near = wide_input(gate_near, up_near)
    near, gate_near, n2_near, *dy_far = tie(near, gate_near, n2_near, *dy_far)
    near = core_give(near)
    dy_far = stacked(*dy_far)
    gate_far, up_far = wide_backward(dy_far, *forward_far[1:])
    gate_far, up_far, dy_far, n2_near, *near = tie(gate_far, up_far, dy_far, n2_near, *near)
    near = first_give(added(*near))
    hidden_near, hidden_far = forward_near[0], forward_far[0]
    grad_down = (down_part + mm_t(hidden_far, dy_far)).astype(BF)
    down_low = low_sum(grad_down, 1)
    far = wide_input(gate_far, up_far)
    far, grad_down, n2_far, n2_near, *near = tie(far, grad_down, n2_far, n2_near, *near)
    far = core_give(far)
    near = last_give(*near)
    gate_near, hidden_near, n2_near, down_low, *rest = tie(gate_near, hidden_near, n2_near, down_low, *far, *near)
    far, near = packed(rest, 2, 4)
    near = reduced(*near)
    far = first_give(added(*far))
    down_keep, down_give = swap(down_low, 1)
    down_come = pair(down_give)
    near, gate_near, hidden_near, n2_far, n2_near, *far = tie(near, gate_near, hidden_near, n2_far, n2_near, *far)
    far = last_give(*far)
    n2_near, n2_far, up_near, gate_near, hidden_near, down_keep, down_come, *far = tie(
        n2_near, n2_far, up_near, gate_near, hidden_near, down_keep, down_come, *far
    )

    far = pair(reduced(*far))
    down_keep = ctx_two(down_keep)
    grad_gate_w = (mm_t(n2_near, gate_near) + mm_t(n2_far, gate_far)).astype(BF)
    middle = n1.shape[0] // 2
    result_keep, result_give = [
        mm(stacked(hidden_near[part], hidden_far[part]), down_full).astype(BF)
        for part in (slice(None, middle), slice(middle, None))
    ]
    far, grad_gate_w, up_near, n2_near, n2_far, result_keep, result_give, *down_keep = tie(
        far, grad_gate_w, up_near, n2_near, n2_far, result_keep, result_give, *down_keep
    )
    gate_low = low_give(grad_gate_w, 0)
    grad_n2 = unfolded(near.astype(F32) + far.astype(F32))
    back2, grad_norm2 = norm_backward(unit2, factor2, gain2_full, grad_n2)
    grad_h1 = seed.astype(F32) + back2
    dh1 = last_ask(*first_ask(grad_h1.astype(BF)))
    grad_up_w = (mm_t(n2_near, up_near) + mm_t(n2_far, up_far)).astype(BF)
    result = added(result_keep, flip(result_give, "ctx", 1, n_ctx))
    grad_up_w, result, *rest = tie(grad_up_w, result, *dh1, *gate_low)
    dh1, gate_low = packed(rest, 4, 2)

    dh1_own = joined(*dh1)
    dh1_come = flip(dh1_own, "ctx", 1, n_ctx)
    up_low = low_give(grad_up_w, 0)
    down_keep = core_two(down_keep)
    mixed_own, out_own = mm(dh1_own, out_full).astype(BF), mm_t(mixed[:middle], dh1_own)
    result, dh1_come, mixed_own, out_own, *rest = tie(result, dh1_come, mixed_own, out_own, *gate_low, *down_keep)
    gate_low, down_keep = packed(rest, 2, 2 * chips)
    result = first_give(result[:middle], result[middle:])
    grad_out = (out_own + mm_t(mixed[middle:], dh1_come)).astype(BF)
    share_out = lax.psum_scatter(grad_out, "shard", scatter_dimension=1, tiled=True)
    dh1_come, grad_out = tie(dh1_come, grad_out)
    gate_keep, gate_give = swap(added(*gate_low), 0)
    grad_mixed = stacked(mixed_own, mm(dh1_come, out_full).astype(BF))
    gate_come = pair(gate_give)
    gate_keep = ctx_two(gate_keep)
    dq, dk, dv = attend_backward(query, key, value, totals, grad_mixed, bias, back_cosine, back_sine)
    dq, dk, dv, gate_come, down_come, *rest = tie(dq, dk, dv, gate_come, down_come, *result, *gate_keep, *up_low)
    result, gate_keep, up_low = packed(rest, 4, chips, 2)
    dqkv = jnp.concatenate([dq, dk, dv], axis=1)
    grad_qkv = mm_t(n1_folded, dqkv).astype(BF)

    dqkv, grad_qkv, gate_come, down_come, share_out, *rest = tie(
        dqkv, grad_qkv, gate_come, down_come, share_out, *result, *up_low, *gate_keep
    )
    result, up_low, gate_keep = packed(rest, 4, 2, chips)
    share_qkv = low_give(grad_qkv, 0)
    grad_n1 = core_give(mm_nt(dqkv, qkv_full).astype(BF))
    up_keep, up_give = swap(added(*up_low), 0)
    up_come = pair(up_give)
    result = last_give(*result)
    three = jnp.stack([gate_come, down_come, up_keep])
    three, *rest = tie(three, *grad_n1, *result, *gate_keep)
    grad_n1, result, gate_keep = packed(rest, 2, 4, chips)
    three, gate_keep = ctx_two(three), core_two(gate_keep)
    grad_n1 = added(*grad_n1)
    result_near, result_far = added(*result[:2]), pair(added(*result[2:]))
    up_come, grad_n1, result_near, result_far, *rest = tie(
        up_come, grad_n1, result_near, result_far, *share_qkv, *three, *gate_keep, *ctx_two(share_out)
    )
    share_qkv, three, gate_keep, share_out = packed(rest, 2, chips, 2 * chips, chips)
    share_qkv, qkv_give = swap(added(*share_qkv), 0)
    qkv_come = pair(qkv_give)
    grad_n1 = first_give(grad_n1)
    three = core_two(three)
    output = (h1 + unfolded(result_near.astype(F32) + result_far.astype(F32))).astype(BF)
    up_come, output, *rest = tie(up_come, output, *grad_n1, *three)
    grad_n1, three = packed(rest, 4, 2 * chips)
    grad_n1 = last_give(*grad_n1)
    up_come, output = ctx_two(up_come), tp_ask(output, 0)
    (grad_g,) = place(
        [(v[None], 0) for v in gate_keep] + [(v, 0) for v in three], both_halves, 2 * n_ctx, 1, 1
    )
    (grad_d,) = place(
        [(v[None], 0) for v in down_keep] + [(v, 1) for v in three], both_halves, 2 * n_ctx, 1, 0
    )
    qkv_come, share_qkv, grad_g, grad_d, *rest = tie(
        qkv_come, share_qkv, grad_g, grad_d, *grad_n1, *up_come, *output
    )
    grad_n1, up_come, output = packed(rest, 4, chips, 2)
    share_qkv = ctx_two(added(share_qkv, qkv_come))
    back1, grad_norm1 = norm_backward(unit1, factor1, gain1_full, reduced(*grad_n1).astype(F32))
    input_grad, output = tp_ask((grad_h1 + back1).astype(BF), 0), as_placed(stacked(*output))
    norms = jnp.stack([grad_norm1, grad_norm2]).reshape(-1, 128)

    def met(values, axis, bits, size):
        for bit in bits:
            values = values + flip(values, axis, bit, size)
        return values

    norms, up_come = met(norms, "tp", tp_bits, n_tp), core_two(up_come)
    norms, output, *rest = tie(norms, output, *share_qkv, *input_grad, *up_come)
    share_qkv, input_grad, up_come = packed(rest, chips, 2, 2 * chips)
    norms, share_qkv, share_out = met(norms, "ctx", [1], n_ctx), core_two(share_qkv), core_two(share_out)
    norms, *rest = tie(norms, *share_qkv, *share_out)
    share_qkv, share_out = packed(rest, 2 * chips, 2 * chips)
    norms = met(norms, "ctx", far_bits, n_ctx)
    input_grad = as_placed(stacked(*input_grad))
    grad_q, grad_k, grad_v = place([(v[None], 0) for v in share_qkv], owners, n_ctx, 3, 1)
    grad_q, grad_k, grad_v, norms = tie(grad_q, grad_k, grad_v, norms)
    norms = met(norms, "shard", low_bits, n_shard)
    (grad_u,) = place([(v, 2) for v in three] + [(v[None], 0) for v in up_come], both_halves, 2 * n_ctx, 1, 1)
    grad_u, norms = tie(grad_u, norms)
    norms = met(norms, "shard", [top], n_shard)
    (grad_o,) = place([(v[None], 0) for v in share_out], owners, n_ctx, 1, 0)
    norms = lax.dynamic_slice_in_dim(norms.reshape(2, width), z * block, block, axis=1)
    return (output, input_grad, norms[0], grad_q, grad_k, grad_v, grad_o, norms[1], grad_g, grad_u, grad_d)


def solution(mesh):
    n_shard, n_ctx, n_tp = mesh.shape["shard"], mesh.shape["ctx"], mesh.shape["tp"]

    def local(*arguments):
        return body(n_shard, n_ctx, n_tp, *arguments)

    return jax.shard_map(
        local,
        mesh=mesh,
        in_specs=(
            P("shard", "ctx", None),
            P("shard", None),
            P("shard"),
            P("shard", "tp"),
            P("shard", "tp"),
            P("shard", "tp"),
            P("tp", "shard"),
            P("shard"),
            P("shard", "tp"),
            P("shard", "tp"),
            P("tp", "shard"),
            P("shard", "ctx", None),
        ),
        out_specs=(
            P("shard", "ctx", None),
            P("shard", "ctx", None),
            P("shard"),
            P("shard", "tp"),
            P("shard", "tp"),
            P("shard", "tp"),
            P("tp", "shard"),
            P("shard"),
            P("shard", "tp"),
            P("shard", "tp"),
            P("tp", "shard"),
        ),
        check_vma=False,
    )
```
